32 devices in a mesh: rep: 2 (over y), grid: 4 (over z), member: 4 (over x, core).
Axes of the slice: x: 2, y: 2, z: 4, core: 2. Of those that a mesh axis runs over, the one named last changes fastest.
Arguments:
- latent: bfloat16 [2, 4, 1024, 2048], P(None, 'member', None, ('rep', 'grid')), parts along dimension 3, may hold values from -6 to 6
- targets: float32 [2, 100, 2048], P(None, None, ('rep', 'grid')), parts along dimension 2, may hold values from -6 to 6
- w1: bfloat16 [768, 1024], P('grid'), may hold values from -0.1875 to 0.1875
- w2: bfloat16 [100, 768], P(None, 'grid'), may hold values from -0.21875 to 0.21875
- noise_table: float32 [4, 768], replicated, may hold values from -6 to 6
- member_ids: int32 [8], P(('rep', 'member')), parts along dimension 0, may hold values from 0 to 3, each once
- lat_weight: float32 [48], replicated, may hold values from 0.1 to 1
- area_index: int32 [2048], P(('rep', 'grid')), parts along dimension 0, may hold values from 0 to 47
- var_weight: float32 [100], replicated, may hold values from 0.2 to 2
Outputs:
- loss: float32 [2], P('rep'), parts along dimension 0
- latent_grad: bfloat16 [2, 4, 1024, 2048], P(None, 'member', None, ('rep', 'grid')), parts along dimension 3
- w1_grad: float32 [1536, 1024], P(('rep', 'grid')), parts along dimension 0
- w2_grad: float32 [100, 1536], P(None, ('rep', 'grid')), parts along dimension 1
The draws below stay inside these ranges and needn't reach their ends.
There are 2 independent parts, one for each index of `rep`. The reference program is written for one: setup_inputs(seed, part) draws one part's arguments, and reference() takes and returns one part's arrays. A program takes and returns all parts, laid end to end along the dimension named above; an argument that names none is the same for every part. Nothing has to cross between parts.
Inputs may be any that keep to these rules, and one draw needn't show every extreme that they name: `member_ids`: each member slot names a different embedding row.
All inputs are finite; a program needn't handle non-finite values.
Results may differ from the reference program's by a relative error of at most 0.011.
The reference program's roundings to bfloat16 on the way (of `hidden`, `cotangent` and `back_before`) count: a program that leaves them out, or rounds other values in their place, can miss the bound.
Values may be sent and summed in bfloat16 or wider, within the bound.
A program may use at most 64 MiB of HBM per device.

```python
import math
import jax
import jax.numpy as jnp

LAT = 1024
HID = 768
VARS = 100
STEPS = 2
NLAT = 48
MEMBERS = 4
NPOINTS = 1024


def place_ends(result, own_key, least, top_value):
    dims = result.shape
    index_at = [jax.random.randint(jax.random.fold_in(own_key, axis), (), 0, dims[axis]) for axis in range(len(dims))]
    result = result.at[tuple(index_at)].set(least)
    longest = dims.index(max(dims))
    index_at[longest] = (index_at[longest] + 1) % dims[longest]
    return result.at[tuple(index_at)].set(top_value)


def levels(key, shape, cuts, smallest, top_value):
    gain, own = 1.0, jax.random.fold_in(key, 6)
    for dim, blocks in cuts:
        steps = jnp.exp(jax.random.uniform(jax.random.fold_in(own, dim), (blocks,), jnp.float32, smallest / len(cuts), top_value / len(cuts)))
        gain = gain * jnp.repeat(steps, shape[dim] // blocks).reshape([-1 if axis == dim else 1 for axis in range(len(shape))])
    return gain


def scatter_about(rng, dims, deviation, reach, pieces=(), held_as=jnp.bfloat16):
    array = jax.random.normal(rng, dims, jnp.float32) * deviation
    if len(pieces) > 0:
        array = levels(rng, dims, pieces, -0.22, 0.18) * array
    return jnp.clip(array, min=-reach, max=reach).astype(held_as)


def setup_inputs(seed: int = 0, part: int = 0) -> dict:
    keys = jax.random.split(jax.random.key(seed), 10)
    own_keys = jax.random.split(jax.random.fold_in(keys[9], part), 10)
    return {
        "latent": scatter_about(own_keys[0], (STEPS, MEMBERS, LAT, NPOINTS), 1.0, 6.0, ((1, 4), (3, 4))),
        "targets": scatter_about(own_keys[1], (STEPS, VARS, NPOINTS), 1.0, 6.0, ((2, 4),), jnp.float32),
        "w1": scatter_about(keys[2], (HID, LAT), LAT ** -0.5, 0.1875, ((0, 4),)),
        "w2": scatter_about(keys[3], (VARS, HID), HID ** -0.5, 0.21875, ((1, 4),)),
        "noise_table": scatter_about(keys[4], (MEMBERS, HID), 1.0, 6.0, (), jnp.float32),
        "member_ids": jax.random.permutation(own_keys[5], MEMBERS).astype(jnp.int32),
        "lat_weight": jnp.clip(jnp.exp(jax.random.uniform(keys[6], (NLAT,), jnp.float32, math.log(0.1), math.log(1.0))), 0.1, 1.0),
        "area_index": place_ends(jax.random.randint(own_keys[7], (NPOINTS,), 0, NLAT), jax.random.fold_in(own_keys[7], 1), 0, NLAT - 1).astype(jnp.int32),
        "var_weight": jnp.clip(jnp.exp(jax.random.uniform(keys[8], (VARS,), jnp.float32, math.log(0.2), math.log(2.0))), 0.2, 2.0),
    }


alpha_fair = 0.95
smooth_width = 0.05
loss_scale = 64.0
grad_shrink = 1.0 / 1024.0

def smooth_abs(diff):
    return jnp.sqrt(diff * diff + smooth_width * smooth_width) - smooth_width

def smooth_sign(diff):
    return diff / jnp.sqrt(diff * diff + smooth_width * smooth_width)

def reference(latent, targets, w1, w2, noise_table, member_ids, lat_weight, area_index, var_weight):
    steps = latent.shape[0]
    members = latent.shape[1]
    variables = targets.shape[1]
    total_points = latent.shape[3]
    fairness = (1.0 - alpha_fair) / members
    pair_coef = (1.0 - fairness) / (members * (members - 1))
    area = jnp.take(lat_weight, area_index, axis=0)
    area_total = jnp.sum(area)
    noise = jnp.take(noise_table, member_ids, axis=0)
    weight = var_weight[:, None] * area[None, :]

    def forward(step, member):
        before = jnp.dot(w1, latent[step, member], preferred_element_type=jnp.float32) + noise[member][:, None]
        return (before, jax.nn.gelu(before).astype(jnp.bfloat16))
    fields = [[jnp.dot(w2, forward(step, member)[1], preferred_element_type=jnp.float32) for member in range(members)] for step in range(steps)]
    scale = total_points / area_total
    loss_total = jnp.zeros((), jnp.float32)
    grad_first = jnp.zeros(w1.shape, jnp.float32)
    grad_second = jnp.zeros(w2.shape, jnp.float32)
    latent_rows = []
    for step in range(steps):
        member_rows = []
        for member in range(members):
            own = fields[step][member]
            error = own - targets[step]
            pair_loss = jnp.zeros_like(own)
            pair_grad = jnp.zeros_like(own)
            for other in range(members):
                spread = own - fields[step][other]
                pair_loss = pair_loss + smooth_abs(spread)
                pair_grad = pair_grad + smooth_sign(spread)
            term = smooth_abs(error) / members - 0.5 * pair_coef * pair_loss
            loss_total = loss_total + jnp.sum(weight * term)
            cotangent = (loss_scale * weight * (smooth_sign(error) / members - pair_coef * pair_grad)).astype(jnp.bfloat16)
            before, hidden = forward(step, member)
            back_hidden = jnp.dot(w2.T, cotangent, preferred_element_type=jnp.float32)
            unused, pullback = jax.vjp(jax.nn.gelu, before)
            back_before = pullback(back_hidden)[0].astype(jnp.bfloat16)
            back_input = jnp.dot(w1.T, back_before, preferred_element_type=jnp.float32)
            member_rows.append((back_input * scale).astype(jnp.bfloat16))
            grad_first = grad_first + jnp.dot(back_before, latent[step, member].T, preferred_element_type=jnp.float32)
            grad_second = grad_second + jnp.dot(cotangent, hidden.T, preferred_element_type=jnp.float32)
        latent_rows.append(jnp.stack(member_rows, axis=0))
    latent_grad = jnp.stack(latent_rows, axis=0)
    loss = jnp.reshape(loss_total / (area_total * steps * variables), (1,))
    return (loss, latent_grad, grad_first * (scale * grad_shrink), grad_second * (scale * grad_shrink))
```

```python
import functools
import math

import jax
import jax.numpy as jnp
from jax import lax
from jax.experimental import pallas as pl
from jax.experimental.pallas import tpu as pltpu
from jax.sharding import PartitionSpec as P

alpha_fair = 0.95
smooth_width = 0.05
loss_scale = 64.0
grad_shrink = 1.0 / 1024.0


def smooth_abs(diff):
    return jnp.sqrt(diff * diff + smooth_width * smooth_width) - smooth_width


def smooth_sign(diff):
    return diff / jnp.sqrt(diff * diff + smooth_width * smooth_width)


def on_device(latent, targets, w1, w2, noise_table, member_ids, lat_weight, area_index, var_weight):
    members = lax.axis_size("member")
    grid_count = lax.axis_size("grid")
    inputs = latent[:, 0]
    steps = inputs.shape[0]
    points = inputs.shape[2]
    variables = targets.shape[1]
    total_points = points * grid_count
    fairness = (1.0 - alpha_fair) / members
    pair_coef = (1.0 - fairness) / (members * (members - 1))
    lookup = (jnp.arange(lat_weight.shape[0])[:, None] == area_index[None, :]).astype(jnp.float32)
    area = jnp.sum(lookup * lat_weight[:, None], axis=0)
    local_area = jnp.sum(area)
    area_total = lax.psum(local_area, "grid")
    chooser = (jnp.arange(noise_table.shape[0]) == member_ids[0]).astype(jnp.float32)
    noise = jnp.sum(noise_table * chooser[:, None], axis=0)
    before = (
        jnp.einsum(
            "hl,slp->shp",
            lax.all_gather(w1, "grid", axis=0, tiled=True),
            inputs,
            preferred_element_type=jnp.float32,
        )
        + noise[None, :, None]
    )
    hidden = jax.nn.gelu(before).astype(jnp.bfloat16)
    w2_full = lax.all_gather(w2, "grid", axis=1, tiled=True)
    fields = jnp.einsum("vh,shp->svp", w2_full, hidden, preferred_element_type=jnp.float32)
    weight = var_weight[:, None] * area[None, :]
    everyone = lax.all_gather(fields[None], "member", axis=0, tiled=True)
    spread = fields[None] - everyone
    pair_loss = jnp.sum(smooth_abs(spread), axis=0)
    pair_grad = jnp.sum(smooth_sign(spread), axis=0)
    error = fields - targets
    term = smooth_abs(error) / members - 0.5 * pair_coef * pair_loss
    loss_local = jnp.sum(weight[None] * term)
    cotangent = (
        loss_scale * weight[None] * (smooth_sign(error) / members - pair_coef * pair_grad)
    ).astype(jnp.bfloat16)
    back_hidden = jnp.einsum("vh,svp->shp", w2_full, cotangent, preferred_element_type=jnp.float32)
    unused, pullback = jax.vjp(jax.nn.gelu, before)
    back_before = pullback(back_hidden)[0].astype(jnp.bfloat16)
    back_input = jnp.einsum(
        "hl,shp->slp",
        lax.all_gather(w1, "grid", axis=0, tiled=True),
        back_before,
        preferred_element_type=jnp.float32,
    )
    grad_first = jnp.einsum("shp,slp->hl", back_before, inputs, preferred_element_type=jnp.float32)
    grad_second = jnp.einsum("shp,svp->hv", hidden, cotangent, preferred_element_type=jnp.float32)
    grid_sums = (
        lax.psum_scatter(grad_first, "grid", scatter_dimension=0, tiled=True),
        lax.psum_scatter(grad_second, "grid", scatter_dimension=0, tiled=True),
    )
    first_rows, second_rows = lax.psum((grid_sums[0], grid_sums[1]), "member")
    loss_total = lax.psum(loss_local, ("grid", "member"))
    scale = total_points / area_total
    latent_grad = (back_input * scale).astype(jnp.bfloat16)[:, None]
    w1_grad = first_rows * (scale * grad_shrink)
    w2_grad = jnp.transpose(second_rows) * (scale * grad_shrink)
    loss = jnp.reshape(loss_total / (area_total * steps * variables), (1,))
    return (loss, latent_grad, w1_grad, w2_grad)


MESH = pl.DeviceIdType.MESH
GRID = 4
MEMB = 4
TANH_SCALE = math.sqrt(2.0 / math.pi)
CUBIC = 0.044715


def gelu_and_slope(x):
    square = x * x
    t = jnp.tanh(TANH_SCALE * x * (1.0 + CUBIC * square))
    half = 0.5 * (1.0 + t)
    slope = half + 0.5 * x * (1.0 - t * t) * (TANH_SCALE * (1.0 + 3.0 * CUBIC * square))
    return x * half, slope


def pick(index, values):
    result = values[-1]
    for i in range(len(values) - 1):
        result = jnp.where(index == i, values[i], result)
    return result


def dot(a, b, contract):
    return lax.dot_general(a, b, ((contract[:1], contract[1:]), ((), ())), preferred_element_type=jnp.float32)


class Slots:
    def __init__(self):
        self.count = 0

    def take(self, n=1):
        self.count += n
        return self.count - n


SEM = Slots()
AREA, W_RECV, W_LEFT, W_CORE = SEM.take(4), SEM.take(4), SEM.take(1), SEM.take(4)
F_CORE, F_X, F_DIAG = SEM.take(2), SEM.take(2), SEM.take(2)
G_CORE, G_ZR, G_ZL, G_X, G_FIN = SEM.take(4), SEM.take(4), SEM.take(4), SEM.take(1), SEM.take(1)
L_MEM, L_GRID = SEM.take(4), SEM.take(4)


def fused(
    lat_hbm, tgt_hbm, w1_hbm, w2_ref, table_ref, ids_ref, latw_ref, aidx_ref, vw_ref,
    loss_ref, lg_hbm, w1g_hbm, w2g_ref,
    lat, tgt, wx, noise, slope, hid, fall, cot, bb, acc, csend, crecv, zsend, zin, xsend, xrecv, fin, lgv, pad,
    abuf, lmem, lgrid, ss, rs, ls,
):
    g, m = lax.axis_index("grid"), lax.axis_index("member")
    c = lax.rem(m, 2)
    core_peer, x_peer = m + 1 - 2 * c, lax.rem(m + 2, 4)
    diag_peer = lax.rem(core_peer + 2, 4)
    steps, _, feats, points = lat_hbm.shape
    variables = tgt_hbm.shape[1]
    rows = w1_hbm.shape[0]
    half = rows // 2
    fairness = (1.0 - alpha_fair) / MEMB
    pair_coef = (1.0 - fairness) / (MEMB * (MEMB - 1))

    def block(t):
        return pl.ds(pl.multiple_of(t * rows, rows), rows)

    def half_of(t, which):
        return pl.ds(pl.multiple_of(t * rows + which * half, half), half)

    def send(src, dst, s_index, r_index, **where):
        return pltpu.make_async_remote_copy(
            src_ref=src, dst_ref=dst, send_sem=ss.at[s_index], recv_sem=rs.at[r_index],
            device_id={"grid": where.get("grid", g), "member": where.get("member", m), "rep": lax.axis_index("rep")},
            device_id_type=MESH,
        )

    w1_in = pltpu.make_async_copy(w1_hbm, wx.at[block(g), pl.ds(0, feats)], ls.at[0])
    w1_in.start()
    lat_in = pltpu.make_async_copy(lat_hbm.at[:, 0], lat, ls.at[1])
    lat_in.start()
    tgt_in = pltpu.make_async_copy(tgt_hbm, tgt, ls.at[2])
    tgt_in.start()

    barrier = pltpu.get_barrier_semaphore()
    for k in range(1, 4):
        pl.semaphore_signal(barrier, inc=1, device_id={"grid": lax.rem(g + k, 4), "member": m, "rep": lax.axis_index("rep")}, device_id_type=MESH)
        pl.semaphore_signal(barrier, inc=1, device_id={"grid": g, "member": lax.rem(m + k, 4), "rep": lax.axis_index("rep")}, device_id_type=MESH)

    pad[...] = jnp.zeros_like(pad)
    pad[:variables, :rows] = w2_ref[...].astype(jnp.float32)
    wx[block(g), feats:] = jnp.transpose(pad[...])[:rows].astype(jnp.bfloat16)
    w1_in.wait()
    pl.semaphore_wait(barrier, 6)

    own_half = half_of(g, c)
    own_right = send(wx.at[own_half], wx.at[own_half], W_RECV + g, W_RECV + g, grid=jnp.minimum(g + 1, 3))
    own_left = send(wx.at[own_half], wx.at[own_half], W_LEFT, W_RECV + g, grid=jnp.maximum(g - 1, 0))
    pl.when(g < 3)(own_right.start)
    pl.when(g > 0)(own_left.start)

    n_lat = latw_ref.shape[1]
    diagonal = lax.broadcasted_iota(jnp.int32, (n_lat, n_lat), 0) == lax.broadcasted_iota(jnp.int32, (n_lat, n_lat), 1)
    lat_col = jnp.sum(jnp.where(diagonal, latw_ref[...], 0.0), axis=1, keepdims=True)
    lookup = lax.broadcasted_iota(jnp.int32, (n_lat, points), 0) == aidx_ref[...]
    area = jnp.sum(jnp.where(lookup, lat_col, 0.0), axis=0, keepdims=True)
    abuf[pl.ds(g, 1)] = jnp.full((1, 8, 128), jnp.sum(area), jnp.float32)
    area_sends = [
        send(abuf.at[g], abuf.at[g], AREA + k, AREA + g, grid=lax.rem(g + k, 4)) for k in range(1, 4)
    ]
    for copy in area_sends:
        copy.start()
    diagonal = lax.broadcasted_iota(jnp.int32, (variables, variables), 0) == lax.broadcasted_iota(jnp.int32, (variables, variables), 1)
    var_col = jnp.sum(jnp.where(diagonal, vw_ref[...], 0.0), axis=1, keepdims=True)
    weight = var_col * area

    chosen = lax.broadcasted_iota(jnp.int32, table_ref.shape, 0) == ids_ref[0]
    noise_row = jnp.sum(jnp.where(chosen, table_ref[...], 0.0), axis=0, keepdims=True)
    noise[...] = jnp.transpose(jnp.broadcast_to(noise_row, (128, noise_row.shape[1])))
    cot[...] = jnp.zeros_like(cot)
    lat_in.wait()

    fields = [None] * steps
    field_sends = []
    mirrored = g >= 2
    near = jnp.where(mirrored, 3 - g, g)
    w_sends = []
    for j in range(GRID):
        o = pick(near, (j, (1, 0, 2, 3)[j]))
        o = jnp.where(mirrored, 3 - o, o)
        if j > 0:
            mine, other = half_of(o, c), half_of(o, 1 - c)
            send(wx.at[mine], wx.at[mine], W_RECV + o, W_RECV + o).wait_recv()
            to_core = send(wx.at[mine], wx.at[mine], W_CORE + o, W_CORE + o, member=core_peer)
            to_core.start()
            ahead = jnp.where(o < g, g + 1, g - 1)
            valid = jnp.logical_and(ahead >= 0, ahead < GRID)
            onward = send(wx.at[mine], wx.at[mine], W_RECV + o, W_RECV + o, grid=jnp.clip(ahead, 0, 3))
            pl.when(valid)(onward.start)
            w_sends.append((to_core, onward, valid))
            send(wx.at[other], wx.at[other], W_CORE + o, W_CORE + o).wait_recv()
        shift = noise[block(o), :]
        shift = jnp.concatenate([shift] * (points // 128), axis=1)
        for s in range(steps):
            before = dot(wx[block(o), :feats], lat[s], (1, 0)) + shift
            value, grad = gelu_and_slope(before)
            value = value.astype(jnp.bfloat16)
            cols = slice(s * points, (s + 1) * points)
            slope[block(o), cols] = grad
            hid[block(o), cols] = value
            part = dot(wx[block(o), feats:], value, (0, 0))
            fields[s] = part if j == 0 else fields[s] + part
            if j == GRID - 1:
                fall[pl.ds(m, 1), s] = fields[s][None, : fall.shape[2]]
                mine = fall.at[m, s]
                pair = (
                    send(mine, mine, F_X + s, F_X + s, member=x_peer),
                    send(mine, mine, F_CORE + s, F_CORE + s, member=core_peer),
                )
                for copy in pair:
                    copy.start()
                field_sends.extend(pair)

    tgt_in.wait()
    for k in range(1, 4):
        o = lax.rem(g + k, 4)
        send(abuf.at[o], abuf.at[o], AREA + k, AREA + o).wait_recv()
    area_total = abuf[0] + abuf[1] + abuf[2] + abuf[3]
    area_total = area_total[:1, :1]
    scale = (points * GRID) / area_total

    for s in range(steps):
        theirs = fall.at[x_peer, s]
        send(theirs, theirs, F_X + s, F_X + s).wait_recv()
        onward = send(theirs, theirs, F_DIAG + s, F_DIAG + s, member=core_peer)
        onward.start()
        field_sends.append(onward)
    loss_sum = jnp.zeros((1, 1), jnp.float32)
    for s in range(steps):
        cols = slice(s * points, (s + 1) * points)
        own = fields[s][:variables]
        error = own - tgt[s]
        root = jnp.sqrt(error * error + smooth_width * smooth_width)
        term = (root - smooth_width) / MEMB
        grad = error / root / MEMB
        near_ref = fall.at[core_peer, s]
        send(near_ref, near_ref, F_CORE + s, F_CORE + s).wait_recv()
        far_ref = fall.at[diag_peer, s]
        for peer in (x_peer, core_peer, diag_peer):
            if peer is diag_peer:
                send(far_ref, far_ref, F_DIAG + s, F_DIAG + s).wait_recv()
            spread = own - fall[pl.ds(peer, 1), s][0, :variables]
            root = jnp.sqrt(spread * spread + smooth_width * smooth_width)
            term = term - (0.5 * pair_coef) * (root - smooth_width)
            grad = grad - pair_coef * (spread / root)
        loss_sum = loss_sum + jnp.sum(weight * term)
        cot[:variables, cols] = (loss_scale * weight * grad).astype(jnp.bfloat16)
        bb[:, cols] = (dot(wx[:, feats:], cot[:, cols], (1, 0)) * slope[:, cols]).astype(jnp.bfloat16)

    lmem[pl.ds(m, 1)] = jnp.broadcast_to(loss_sum, (1, 8, 128))
    late = [send(lmem.at[m], lmem.at[m], L_MEM + k, L_MEM + m, member=lax.rem(m + k, 4)) for k in range(1, 4)]
    for copy in late:
        copy.start()

    order = [
        pick(g, (3, 3, 0, 0)),
        pick(g, (2, 0, 3, 1)),
        pick(g, (1, 2, 1, 2)),
        g,
    ]
    for j, t in enumerate(order):
        first = dot(bb[block(t), :points], lat[0], (1, 1))
        for s in range(1, steps):
            first = first + dot(bb[block(t), s * points : (s + 1) * points], lat[s], (1, 1))
        second = dot(hid[block(t), :], cot[...], (1, 1))
        for which in range(2):
            part = slice(which * half, (which + 1) * half)

            @pl.when(c == which)
            def _():
                acc[j, :, :feats] = first[part]
                acc[j, :, feats:] = second[part]

            @pl.when(c != which)
            def _():
                csend[j, :, :feats] = first[part].astype(jnp.bfloat16)
                csend[j, :, feats:] = second[part].astype(jnp.bfloat16)

        copy = send(csend.at[j], crecv.at[j], G_CORE + j, G_CORE + j, member=core_peer)
        copy.start()
        late.append(copy)

    def back_input(s, piece):
        cols = slice(s * points, (s + 1) * points)
        span = slice(piece * 256, (piece + 1) * 256)
        lgv[s, span] = (dot(wx[:, span], bb[:, cols], (0, 0)) * scale).astype(jnp.bfloat16)

    pieces = [(s, p) for s in range(steps) for p in range(feats // 256)]
    share = -(-len(pieces) // 3)
    z_sends = []
    for j, t in enumerate(order):
        send(csend.at[j], crecv.at[j], G_CORE + j, G_CORE + j).wait_recv()
        total = acc[j] + crecv[j].astype(jnp.float32)
        from_left = jnp.logical_and(g > 0, t >= g)
        from_right = jnp.logical_and(g < 3, t <= g)
        acc[j] = total
        for present, base, side in ((from_left, G_ZR, 0), (from_right, G_ZL, 1)):

            @pl.when(present)
            def _():
                send(zin.at[side, t], zin.at[side, t], base + t, base + t).wait_recv()
                acc[j] = acc[j] + zin[side, pl.ds(t, 1)][0].astype(jnp.float32)

        if j < GRID - 1:
            zsend[j] = acc[j].astype(jnp.bfloat16)
            right = send(zsend.at[j], zin.at[0, t], G_ZR + j, G_ZR + t, grid=jnp.minimum(g + 1, 3))
            left = send(zsend.at[j], zin.at[1, t], G_ZL + j, G_ZL + t, grid=jnp.maximum(g - 1, 0))
            pl.when(t > g)(right.start)
            pl.when(t < g)(left.start)
            z_sends.append((right, t > g, left, t < g))
            for s, p in pieces[j * share : (j + 1) * share]:
                back_input(s, p)
            if j == 0:
                for k in range(1, 4):
                    o = lax.rem(m + k, 4)
                    send(lmem.at[o], lmem.at[o], L_MEM + k, L_MEM + o).wait_recv()
                lgrid[pl.ds(g, 1)] = (lmem[0] + lmem[1] + lmem[2] + lmem[3])[None]
                for k in range(1, 4):
                    copy = send(lgrid.at[g], lgrid.at[g], L_GRID + k, L_GRID + g, grid=lax.rem(g + k, 4))
                    copy.start()
                    late.append(copy)
            if j == GRID - 2:
                lg_out = pltpu.make_async_copy(lgv, lg_hbm.at[:, 0], ls.at[3])
                lg_out.start()
                for k in range(1, 4):
                    o = lax.rem(g + k, 4)
                    send(lgrid.at[o], lgrid.at[o], L_GRID + k, L_GRID + o).wait_recv()
                loss_total = lgrid[0] + lgrid[1] + lgrid[2] + lgrid[3]
                loss_ref[...] = loss_total[:1, :1] / (area_total * (steps * variables))

    xsend[...] = acc[GRID - 1].astype(jnp.bfloat16)
    copy = send(xsend, xrecv, G_X, G_X, member=x_peer)
    copy.start()
    late.append(copy)
    copy.wait_recv()
    mine, other = half_of(0, c), half_of(0, 1 - c)
    fin[mine] = (xsend[...].astype(jnp.float32) + xrecv[...].astype(jnp.float32)) * (scale * grad_shrink)
    copy = send(fin.at[mine], fin.at[mine], G_FIN, G_FIN, member=core_peer)
    copy.start()
    mine_out = pltpu.make_async_copy(fin.at[mine, pl.ds(0, feats)], w1g_hbm.at[mine], ls.at[4])
    mine_out.start()
    send(fin.at[other], fin.at[other], G_FIN, G_FIN).wait_recv()
    other_out = pltpu.make_async_copy(fin.at[other, pl.ds(0, feats)], w1g_hbm.at[other], ls.at[5])
    other_out.start()
    pad[:, :rows] = jnp.transpose(
        jnp.concatenate([fin[:, feats:], jnp.zeros((pad.shape[1] - rows, 128), jnp.float32)], axis=0)
    )[:, :rows]
    w2g_ref[...] = pad[:variables, :rows]

    pl.when(g < 3)(own_right.wait_send)
    pl.when(g > 0)(own_left.wait_send)
    for to_core, onward, valid in w_sends:
        to_core.wait_send()
        pl.when(valid)(onward.wait_send)
    for copy in area_sends + field_sends + late + [copy]:
        copy.wait_send()
    for right, go_right, left, go_left in z_sends:
        pl.when(go_right)(right.wait_send)
        pl.when(go_left)(left.wait_send)
    lg_out.wait()
    mine_out.wait()
    other_out.wait()


def fused_on_device(latent, targets, w1, w2, noise_table, member_ids, lat_weight, area_index, var_weight):
    steps, _, feats, points = latent.shape
    variables = targets.shape[1]
    rows = w1.shape[0]
    hidden = rows * GRID
    half = rows // 2
    wide = feats + 128
    padded = -(-variables // 8) * 8
    f32, bf16 = jnp.float32, jnp.bfloat16
    hbm, vmem = pl.BlockSpec(memory_space=pl.ANY), pl.BlockSpec(memory_space=pltpu.VMEM)
    smem = pl.BlockSpec(memory_space=pltpu.SMEM)
    loss, latent_grad, w1_grad, w2_grad = pl.pallas_call(
        fused,
        out_shape=(
            jax.ShapeDtypeStruct((1, 1), f32),
            jax.ShapeDtypeStruct(latent.shape, bf16),
            jax.ShapeDtypeStruct((rows, feats), f32),
            jax.ShapeDtypeStruct((variables, rows), f32),
        ),
        in_specs=[hbm, hbm, hbm, vmem, vmem, smem, vmem, vmem, vmem],
        out_specs=(vmem, hbm, hbm, vmem),
        scratch_shapes=[
            pltpu.VMEM((steps, feats, points), bf16),
            pltpu.VMEM((steps, variables, points), f32),
            pltpu.VMEM((hidden, wide), bf16),
            pltpu.VMEM((hidden, 128), f32),
            pltpu.VMEM((hidden, steps * points), f32),
            pltpu.VMEM((hidden, steps * points), bf16),
            pltpu.VMEM((MEMB, steps, padded, points), f32),
            pltpu.VMEM((128, steps * points), bf16),
            pltpu.VMEM((hidden, steps * points), bf16),
            pltpu.VMEM((GRID, half, wide), f32),
            pltpu.VMEM((GRID, half, wide), bf16),
            pltpu.VMEM((GRID, half, wide), bf16),
            pltpu.VMEM((GRID - 1, half, wide), bf16),
            pltpu.VMEM((2, GRID, half, wide), bf16),
            pltpu.VMEM((half, wide), bf16),
            pltpu.VMEM((half, wide), bf16),
            pltpu.VMEM((rows, wide), f32),
            pltpu.VMEM((steps, feats, points), bf16),
            pltpu.VMEM((128, 256), f32),
            pltpu.VMEM((GRID, 8, 128), f32),
            pltpu.VMEM((MEMB, 8, 128), f32),
            pltpu.VMEM((GRID, 8, 128), f32),
            pltpu.SemaphoreType.DMA((SEM.count,)),
            pltpu.SemaphoreType.DMA((SEM.count,)),
            pltpu.SemaphoreType.DMA((6,)),
        ],
        compiler_params=pltpu.CompilerParams(
            collective_id=0, has_side_effects=True, vmem_limit_bytes=48 * 1024 * 1024
        ),
        cost_estimate=pl.CostEstimate(
            flops=6 * hidden * feats * steps * points, bytes_accessed=4 * 1024 * 1024, transcendentals=hidden * steps * points
        ),
    )(
        latent, targets, w1, w2, noise_table, member_ids,
        lat_weight[None, :], area_index[None, :], var_weight[None, :],
    )
    return jnp.reshape(loss, (1,)), latent_grad, w1_grad, w2_grad


def solution(mesh):
    return jax.shard_map(
        on_device if tuple(mesh.shape[a] for a in ("grid", "member")) != (4, 4) else fused_on_device,
        mesh=mesh,
        in_specs=(
            P(None, "member", None, ("rep", "grid")),
            P(None, None, ("rep", "grid")),
            P("grid", None),
            P(None, "grid"),
            P(),
            P(("rep", "member")),
            P(),
            P(("rep", "grid")),
            P(),
        ),
        out_specs=(
            P("rep"),
            P(None, "member", None, ("rep", "grid")),
            P(("rep", "grid"), None),
            P(None, ("rep", "grid")),
        ),
        check_vma=False,
    )
```

```python
import functools
import math

import jax
import jax.numpy as jnp
from jax import lax
from jax.experimental import pallas as pl
from jax.experimental.pallas import tpu as pltpu
from jax.sharding import PartitionSpec as P

alpha_fair = 0.95
smooth_width = 0.05
loss_scale = 64.0
grad_shrink = 1.0 / 1024.0


def smooth_abs(diff):
    return jnp.sqrt(diff * diff + smooth_width * smooth_width) - smooth_width


def smooth_sign(diff):
    return diff / jnp.sqrt(diff * diff + smooth_width * smooth_width)


def on_device(latent, targets, w1, w2, noise_table, member_ids, lat_weight, area_index, var_weight):
    members = lax.axis_size("member")
    grid_count = lax.axis_size("grid")
    inputs = latent[:, 0]
    steps = inputs.shape[0]
    points = inputs.shape[2]
    variables = targets.shape[1]
    total_points = points * grid_count
    fairness = (1.0 - alpha_fair) / members
    pair_coef = (1.0 - fairness) / (members * (members - 1))
    lookup = (jnp.arange(lat_weight.shape[0])[:, None] == area_index[None, :]).astype(jnp.float32)
    area = jnp.sum(lookup * lat_weight[:, None], axis=0)
    local_area = jnp.sum(area)
    area_total = lax.psum(local_area, "grid")
    chooser = (jnp.arange(noise_table.shape[0]) == member_ids[0]).astype(jnp.float32)
    noise = jnp.sum(noise_table * chooser[:, None], axis=0)
    before = (
        jnp.einsum(
            "hl,slp->shp",
            lax.all_gather(w1, "grid", axis=0, tiled=True),
            inputs,
            preferred_element_type=jnp.float32,
        )
        + noise[None, :, None]
    )
    hidden = jax.nn.gelu(before).astype(jnp.bfloat16)
    w2_full = lax.all_gather(w2, "grid", axis=1, tiled=True)
    fields = jnp.einsum("vh,shp->svp", w2_full, hidden, preferred_element_type=jnp.float32)
    weight = var_weight[:, None] * area[None, :]
    everyone = lax.all_gather(fields[None], "member", axis=0, tiled=True)
    spread = fields[None] - everyone
    pair_loss = jnp.sum(smooth_abs(spread), axis=0)
    pair_grad = jnp.sum(smooth_sign(spread), axis=0)
    error = fields - targets
    term = smooth_abs(error) / members - 0.5 * pair_coef * pair_loss
    loss_local = jnp.sum(weight[None] * term)
    cotangent = (
        loss_scale * weight[None] * (smooth_sign(error) / members - pair_coef * pair_grad)
    ).astype(jnp.bfloat16)
    back_hidden = jnp.einsum("vh,svp->shp", w2_full, cotangent, preferred_element_type=jnp.float32)
    unused, pullback = jax.vjp(jax.nn.gelu, before)
    back_before = pullback(back_hidden)[0].astype(jnp.bfloat16)
    back_input = jnp.einsum(
        "hl,shp->slp",
        lax.all_gather(w1, "grid", axis=0, tiled=True),
        back_before,
        preferred_element_type=jnp.float32,
    )
    grad_first = jnp.einsum("shp,slp->hl", back_before, inputs, preferred_element_type=jnp.float32)
    grad_second = jnp.einsum("shp,svp->hv", hidden, cotangent, preferred_element_type=jnp.float32)
    grid_sums = (
        lax.psum_scatter(grad_first, "grid", scatter_dimension=0, tiled=True),
        lax.psum_scatter(grad_second, "grid", scatter_dimension=0, tiled=True),
    )
    first_rows, second_rows = lax.psum((grid_sums[0], grid_sums[1]), "member")
    loss_total = lax.psum(loss_local, ("grid", "member"))
    scale = total_points / area_total
    latent_grad = (back_input * scale).astype(jnp.bfloat16)[:, None]
    w1_grad = first_rows * (scale * grad_shrink)
    w2_grad = jnp.transpose(second_rows) * (scale * grad_shrink)
    loss = jnp.reshape(loss_total / (area_total * steps * variables), (1,))
    return (loss, latent_grad, w1_grad, w2_grad)


MESH = pl.DeviceIdType.MESH
GRID = 4
MEMB = 4
TANH_SCALE = math.sqrt(2.0 / math.pi)
CUBIC = 0.044715


def gelu_and_slope(x):
    square = x * x
    t = jnp.tanh(TANH_SCALE * x * (1.0 + CUBIC * square))
    half = 0.5 * (1.0 + t)
    slope = half + 0.5 * x * (1.0 - t * t) * (TANH_SCALE * (1.0 + 3.0 * CUBIC * square))
    return x * half, slope


def pick(index, values):
    result = values[-1]
    for i in range(len(values) - 1):
        result = jnp.where(index == i, values[i], result)
    return result


def dot(a, b, contract):
    return lax.dot_general(a, b, ((contract[:1], contract[1:]), ((), ())), preferred_element_type=jnp.float32)


class Slots:
    def __init__(self):
        self.count = 0

    def take(self, n=1):
        self.count += n
        return self.count - n


SEM = Slots()
AREA, W_Z = SEM.take(4), SEM.take(4)
W_PLANE, W_CORE = SEM.take(3 * 4), SEM.take(4 * 4)
F_CORE, F_X, F_DIAG = SEM.take(2), SEM.take(2), SEM.take(2)
G_CORE, G_X, G_Z = SEM.take(4), SEM.take(4), SEM.take(4)
G_ENDX, G_ENDC, G_ENDD = SEM.take(1), SEM.take(1), SEM.take(1)
L_MEM, L_GRID = SEM.take(4), SEM.take(4)
QUART = 4
EXTRA = 16


def fused(
    lat_hbm, tgt_hbm, w1_hbm, w2_ref, table_ref, ids_ref, latw_ref, aidx_ref, vw_ref,
    loss_ref, lg_hbm, w1g_hbm, w2g_ref,
    lat, tgt, wx, noise, slope, hid, fall, cot, bb, gbuf, acc, csend, crecv, xs, xr, zs, zr, fin, finf, lgv, pad,
    abuf, lmem, lgrid, ss, rs, ls,
):
    y, g, m = lax.axis_index("rep"), lax.axis_index("grid"), lax.axis_index("member")
    c = lax.rem(m, 2)
    x = lax.div(m, 2)
    quarter = 2 * x + y
    core_peer, x_peer = m + 1 - 2 * c, lax.rem(m + 2, 4)
    diag_peer = lax.rem(core_peer + 2, 4)
    steps, _, feats, points = lat_hbm.shape
    variables = tgt_hbm.shape[0]
    rows = w1_hbm.shape[0]
    half = rows // 2
    span = feats // QUART
    fairness = (1.0 - alpha_fair) / MEMB
    pair_coef = (1.0 - fairness) / (MEMB * (MEMB - 1))

    def block(t):
        return pl.ds(pl.multiple_of(t * rows, rows), rows)

    def send(src, dst, s_index, r_index, **where):
        return pltpu.make_async_remote_copy(
            src_ref=src, dst_ref=dst, send_sem=ss.at[s_index], recv_sem=rs.at[r_index],
            device_id={"grid": where.get("grid", g), "member": where.get("member", m), "rep": where.get("rep", y)},
            device_id_type=MESH,
        )

    def first_rows(o):
        own = wx[pl.ds(o, 1)][0]
        return jnp.concatenate(
            [jnp.concatenate([own[q, i, :half] for q in range(QUART)], axis=1) for i in range(2)], axis=0
        )

    def second_columns(o):
        own = wx[pl.ds(o, 1)][0]
        return jnp.concatenate([own[q, i, half:] for q in range(QUART) for i in range(2)], axis=0)[:, :rows]

    w1_in = [
        pltpu.make_async_copy(
            w1_hbm.at[pl.ds(i * half, half), pl.ds(q * span, span)], wx.at[g, q, i, pl.ds(0, half)], ls.at[8 + 2 * q + i]
        )
        for q in range(QUART)
        for i in range(2)
    ]
    for copy in w1_in:
        copy.start()
    lat_in = pltpu.make_async_copy(lat_hbm.at[:, 0], lat, ls.at[1])
    lat_in.start()
    tgt_in = [pltpu.make_async_copy(tgt_hbm.at[:, s], tgt.at[s], ls.at[5 + s]) for s in range(steps)]
    for copy in tgt_in:
        copy.start()

    barrier = pltpu.get_barrier_semaphore()

    def greet(**where):
        pl.semaphore_signal(
            barrier, inc=1, device_id_type=MESH,
            device_id={"grid": where.get("grid", g), "member": where.get("member", m), "rep": where.get("rep", y)},
        )

    for k in range(1, 4):
        greet(grid=lax.rem(g + k, 4))
        greet(member=lax.rem(m + k, 4))
    greet(rep=1 - y)
    greet(rep=1 - y, member=x_peer)

    pad[...] = jnp.zeros_like(pad)
    pad[:rows, :variables] = w2_ref[...].astype(jnp.float32)
    second = jnp.transpose(pad[...]).astype(jnp.bfloat16)
    for q in range(QUART):
        for i in range(2):
            at = (2 * q + i) * EXTRA
            wx[pl.ds(g, 1), q, i, half:] = second[None, at : at + EXTRA]
    for copy in w1_in:
        copy.wait()
    pl.semaphore_wait(barrier, 8)

    piece = wx.at[g, quarter, c]
    w_sends = [send(piece, piece, W_Z + k, W_Z + g, grid=lax.rem(g + k, 4)) for k in range(1, 4)]
    for copy in w_sends:
        copy.start()

    n_lat = latw_ref.shape[1]
    diagonal = lax.broadcasted_iota(jnp.int32, (n_lat, n_lat), 0) == lax.broadcasted_iota(jnp.int32, (n_lat, n_lat), 1)
    lat_col = jnp.sum(jnp.where(diagonal, latw_ref[...], 0.0), axis=1, keepdims=True)
    lookup = lax.broadcasted_iota(jnp.int32, (n_lat, points), 0) == aidx_ref[...]
    area = jnp.sum(jnp.where(lookup, lat_col, 0.0), axis=0, keepdims=True)
    abuf[pl.ds(g, 1)] = jnp.full((1, 8, 128), jnp.sum(area), jnp.float32)
    area_sends = [
        send(abuf.at[g], abuf.at[g], AREA + k, AREA + g, grid=lax.rem(g + k, 4)) for k in range(1, 4)
    ]
    for copy in area_sends:
        copy.start()
    diagonal = lax.broadcasted_iota(jnp.int32, (variables, variables), 0) == lax.broadcasted_iota(jnp.int32, (variables, variables), 1)
    var_col = jnp.sum(jnp.where(diagonal, vw_ref[...], 0.0), axis=1, keepdims=True)
    weight = var_col * area

    chosen = lax.broadcasted_iota(jnp.int32, table_ref.shape, 0) == ids_ref[0]
    noise_row = jnp.sum(jnp.where(chosen, table_ref[...], 0.0), axis=0, keepdims=True)
    noise[...] = jnp.transpose(jnp.broadcast_to(noise_row, (128, noise_row.shape[1])))
    cot[...] = jnp.zeros_like(cot)
    lat_in.wait()

    fields = [None] * steps
    field_sends = []
    mirrored = g >= 2
    near = jnp.where(mirrored, 3 - g, g)
    owners = []
    for j in range(GRID):
        o = pick(near, (j, (1, 0, 2, 3)[j]))
        owners.append(jnp.where(mirrored, 3 - o, o))
    plane = ((dict(member=x_peer), 2 * (1 - x) + y), (dict(rep=1 - y), 2 * x + 1 - y),
             (dict(member=x_peer, rep=1 - y), 2 * (1 - x) + 1 - y))

    def spread_piece(o):
        mine = wx.at[o, quarter, c]
        send(mine, mine, W_Z + o, W_Z + o).wait_recv()
        for i, (where, _) in enumerate(plane):
            copy = send(mine, mine, W_PLANE + 4 * i + o, W_PLANE + 4 * i + o, **where)
            copy.start()
            w_sends.append(copy)
        copy = send(mine, mine, W_CORE + 12 + o, W_CORE + 12 + o, member=core_peer)
        copy.start()
        w_sends.append(copy)

    def pass_to_core(o):
        for i, (_, q) in enumerate(plane):
            got = wx.at[o, q, c]
            send(got, got, W_PLANE + 4 * i + o, W_PLANE + 4 * i + o).wait_recv()
            copy = send(got, got, W_CORE + 4 * i + o, W_CORE + 4 * i + o, member=core_peer)
            copy.start()
            w_sends.append(copy)

    def have_block(o):
        for i, q in enumerate([q for _, q in plane] + [quarter]):
            got = wx.at[o, q, 1 - c]
            send(got, got, W_CORE + 4 * i + o, W_CORE + 4 * i + o).wait_recv()

    for j in range(GRID):
        o = owners[j]
        if j == 1:
            for later in owners[1:]:
                spread_piece(later)
        if j > 0:
            pass_to_core(o)
            have_block(o)
        shift = noise[block(o), :]
        shift = jnp.concatenate([shift] * (points // 128), axis=1)
        own_first, own_second = first_rows(o), second_columns(o)
        for s in range(steps):
            before = dot(own_first, lat[s], (1, 0)) + shift
            value, grad = gelu_and_slope(before)
            value = value.astype(jnp.bfloat16)
            cols = slice(s * points, (s + 1) * points)
            slope[block(o), cols] = grad
            hid[block(o), cols] = value
            part = dot(own_second, value, (1, 0))
            fields[s] = part if j == 0 else fields[s] + part
            if j == GRID - 1:
                fall[pl.ds(m, 1), s] = fields[s][None, : fall.shape[2]]
                mine = fall.at[m, s]
                pair = (
                    send(mine, mine, F_X + s, F_X + s, member=x_peer),
                    send(mine, mine, F_CORE + s, F_CORE + s, member=core_peer),
                )
                for copy in pair:
                    copy.start()
                field_sends.extend(pair)

    for copy in tgt_in:
        copy.wait()
    for k in range(1, 4):
        o = lax.rem(g + k, 4)
        send(abuf.at[o], abuf.at[o], AREA + k, AREA + o).wait_recv()
    area_total = abuf[0] + abuf[1] + abuf[2] + abuf[3]
    area_total = area_total[:1, :1]
    scale = (points * GRID) / area_total

    for s in range(steps):
        theirs = fall.at[x_peer, s]
        send(theirs, theirs, F_X + s, F_X + s).wait_recv()
        onward = send(theirs, theirs, F_DIAG + s, F_DIAG + s, member=core_peer)
        onward.start()
        field_sends.append(onward)
    loss_sum = jnp.zeros((1, 1), jnp.float32)
    for s in range(steps):
        cols = slice(s * points, (s + 1) * points)
        own = fields[s][:variables]
        error = own - tgt[s]
        root = jnp.sqrt(error * error + smooth_width * smooth_width)
        term = (root - smooth_width) / MEMB
        grad = error / root / MEMB
        near_ref = fall.at[core_peer, s]
        send(near_ref, near_ref, F_CORE + s, F_CORE + s).wait_recv()
        far_ref = fall.at[diag_peer, s]
        for peer in (x_peer, core_peer, diag_peer):
            if peer is diag_peer:
                send(far_ref, far_ref, F_DIAG + s, F_DIAG + s).wait_recv()
            spread = own - fall[pl.ds(peer, 1), s][0, :variables]
            root = jnp.sqrt(spread * spread + smooth_width * smooth_width)
            term = term - (0.5 * pair_coef) * (root - smooth_width)
            grad = grad - pair_coef * (spread / root)
        loss_sum = loss_sum + jnp.sum(weight * term)
        cot[:variables, cols] = (loss_scale * weight * grad).astype(jnp.bfloat16)
        for o in range(GRID):
            hidden_rows = slice(o * rows, (o + 1) * rows)
            back = dot(second_columns(o), cot[:, cols], (0, 0))
            bb[hidden_rows, cols] = (back * slope[hidden_rows, cols]).astype(jnp.bfloat16)

    lmem[pl.ds(m, 1)] = jnp.broadcast_to(loss_sum, (1, 8, 128))
    late = [send(lmem.at[m], lmem.at[m], L_MEM + k, L_MEM + m, member=lax.rem(m + k, 4)) for k in range(1, 4)]
    for copy in late:
        copy.start()

    order = [
        pick(g, (3, 3, 0, 0)),
        pick(g, (2, 0, 3, 1)),
        pick(g, (1, 2, 1, 2)),
        g,
    ]
    fourth = half // 2
    my_half = pl.ds(pl.multiple_of(c * half, half), half)
    their_half = pl.ds(pl.multiple_of((1 - c) * half, half), half)
    my_fourth = pl.ds(pl.multiple_of(x * fourth, fourth), fourth)
    their_fourth = pl.ds(pl.multiple_of((1 - x) * fourth, fourth), fourth)

    def start(copy):
        copy.start()
        late.append(copy)

    def partial(j):
        t = order[j]
        first = dot(bb[block(t), :points], lat[0], (1, 1))
        for s in range(1, steps):
            first = first + dot(bb[block(t), s * points : (s + 1) * points], lat[s], (1, 1))
        gbuf[j, :, :feats] = first
        gbuf[j, :, feats:] = dot(hid[block(t), :], cot[...], (1, 1))
        csend[j] = gbuf[j, their_half].astype(jnp.bfloat16)
        start(send(csend.at[j], crecv.at[j], G_CORE + j, G_CORE + j, member=core_peer))

    def over_x(j):
        send(csend.at[j], crecv.at[j], G_CORE + j, G_CORE + j).wait_recv()
        acc[...] = gbuf[j, my_half] + crecv[j].astype(jnp.float32)
        xs[j] = acc[their_fourth].astype(jnp.bfloat16)
        gbuf[j, :fourth] = acc[my_fourth]
        start(send(xs.at[j], xr.at[j], G_X + j, G_X + j, member=x_peer))

    def along_z(j):
        send(xs.at[j], xr.at[j], G_X + j, G_X + j).wait_recv()
        total = gbuf[j, :fourth] + xr[j].astype(jnp.float32)
        if j == GRID - 1:
            gbuf[j, :fourth] = total
        else:
            zs[j] = total.astype(jnp.bfloat16)
            start(send(zs.at[j], zr.at[g], G_Z + j, G_Z + g, grid=order[j]))

    def back_input(s, q):
        cols = slice(s * points, (s + 1) * points)
        left = jnp.concatenate([wx[o, q, i, :half] for o in range(GRID) for i in range(2)], axis=0)
        lgv[s, q * span : (q + 1) * span] = (dot(left, bb[:, cols], (0, 0)) * scale).astype(jnp.bfloat16)

    pieces = [(s, q) for s in range(steps) for q in range(QUART)]
    for i in range(GRID + 2):
        if i < GRID:
            partial(i)
        if 0 <= i - 1 < GRID:
            over_x(i - 1)
        if i - 2 >= 0:
            along_z(i - 2)
        if i == 2:
            for k in range(1, 4):
                o = lax.rem(m + k, 4)
                send(lmem.at[o], lmem.at[o], L_MEM + k, L_MEM + o).wait_recv()
            lgrid[pl.ds(g, 1)] = (lmem[0] + lmem[1] + lmem[2] + lmem[3])[None]
            for k in range(1, 4):
                start(send(lgrid.at[g], lgrid.at[g], L_GRID + k, L_GRID + g, grid=lax.rem(g + k, 4)))
        if i >= GRID - 1:
            for s, q in pieces[(i - GRID + 1) * 2 : (i - GRID + 2) * 2]:
                back_input(s, q)
    for s, q in pieces[6:]:
        back_input(s, q)
    lg_out = pltpu.make_async_copy(lgv, lg_hbm.at[:, 0], ls.at[3])
    lg_out.start()
    for k in range(1, 4):
        o = lax.rem(g + k, 4)
        send(lgrid.at[o], lgrid.at[o], L_GRID + k, L_GRID + o).wait_recv()
    loss_total = lgrid[0] + lgrid[1] + lgrid[2] + lgrid[3]
    loss_ref[...] = loss_total[:1, :1] / (area_total * (steps * variables))

    total = gbuf[GRID - 1, :fourth]
    for k in range(1, 4):
        o = lax.rem(g + k, 4)
        send(zr.at[o], zr.at[o], G_Z + k, G_Z + o).wait_recv()
        total = total + zr[pl.ds(o, 1)][0].astype(jnp.float32)
    fin[pl.ds(m, 1)] = (total * (scale * grad_shrink)).astype(jnp.bfloat16)[None]

    def give(o, s_index, peer):
        start(send(fin.at[o], fin.at[o], s_index, s_index, member=peer))

    def got(o, s_index):
        send(fin.at[o], fin.at[o], s_index, s_index).wait_recv()

    def finish(o):
        place = 2 * lax.rem(o, 2) + lax.div(o, 2)
        finf[pl.ds(pl.multiple_of(place * fourth, fourth), fourth)] = fin[pl.ds(o, 1)][0].astype(jnp.float32)
        here = pl.ds(pl.multiple_of(place * fourth, fourth), fourth)
        copy = pltpu.make_async_copy(finf.at[here, pl.ds(0, feats)], w1g_hbm.at[here], ls.at[16 + len(outs)])
        copy.start()
        outs.append(copy)

    outs = []
    give(m, G_ENDX, x_peer)
    give(m, G_ENDC, core_peer)
    finish(m)
    got(core_peer, G_ENDC)
    finish(core_peer)
    got(x_peer, G_ENDX)
    give(x_peer, G_ENDD, core_peer)
    finish(x_peer)
    got(diag_peer, G_ENDD)
    finish(diag_peer)
    w2g_ref[...] = finf[:, feats : feats + variables]

    for copy in w_sends + area_sends + field_sends + late:
        copy.wait_send()
    for copy in outs + [lg_out]:
        copy.wait()


def fused_on_device(latent, targets, w1, w2, noise_table, member_ids, lat_weight, area_index, var_weight):
    steps, _, feats, points = latent.shape
    variables = targets.shape[1]
    rows = w1.shape[0]
    hidden = rows * GRID
    half = rows // 2
    wide = feats + 128
    fourth = half // 2
    padded = -(-variables // 8) * 8
    f32, bf16 = jnp.float32, jnp.bfloat16
    hbm, vmem = pl.BlockSpec(memory_space=pl.ANY), pl.BlockSpec(memory_space=pltpu.VMEM)
    smem = pl.BlockSpec(memory_space=pltpu.SMEM)
    loss, latent_grad, w1_grad, w2_grad = pl.pallas_call(
        fused,
        out_shape=(
            jax.ShapeDtypeStruct((1, 1), f32),
            jax.ShapeDtypeStruct(latent.shape, bf16),
            jax.ShapeDtypeStruct((rows, feats), f32),
            jax.ShapeDtypeStruct((rows, variables), f32),
        ),
        in_specs=[hbm, hbm, hbm, vmem, vmem, smem, vmem, vmem, vmem],
        out_specs=(vmem, hbm, hbm, vmem),
        scratch_shapes=[
            pltpu.VMEM((steps, feats, points), bf16),
            pltpu.VMEM((steps, variables, points), f32),
            pltpu.VMEM((GRID, QUART, 2, half + EXTRA, feats // QUART), bf16),
            pltpu.VMEM((hidden, 128), f32),
            pltpu.VMEM((hidden, steps * points), f32),
            pltpu.VMEM((hidden, steps * points), bf16),
            pltpu.VMEM((MEMB, steps, padded, points), f32),
            pltpu.VMEM((128, steps * points), bf16),
            pltpu.VMEM((hidden, steps * points), bf16),
            pltpu.VMEM((GRID, rows, wide), f32),
            pltpu.VMEM((half, wide), f32),
            pltpu.VMEM((GRID, half, wide), bf16),
            pltpu.VMEM((GRID, half, wide), bf16),
            pltpu.VMEM((GRID, fourth, wide), bf16),
            pltpu.VMEM((GRID, fourth, wide), bf16),
            pltpu.VMEM((GRID - 1, fourth, wide), bf16),
            pltpu.VMEM((GRID, fourth, wide), bf16),
            pltpu.VMEM((MEMB, fourth, wide), bf16),
            pltpu.VMEM((rows, wide), f32),
            pltpu.VMEM((steps, feats, points), bf16),
            pltpu.VMEM((256, 128), f32),
            pltpu.VMEM((GRID, 8, 128), f32),
            pltpu.VMEM((MEMB, 8, 128), f32),
            pltpu.VMEM((GRID, 8, 128), f32),
            pltpu.SemaphoreType.DMA((SEM.count,)),
            pltpu.SemaphoreType.DMA((SEM.count,)),
            pltpu.SemaphoreType.DMA((20,)),
        ],
        compiler_params=pltpu.CompilerParams(
            collective_id=0, has_side_effects=True, vmem_limit_bytes=60 * 1024 * 1024
        ),
        cost_estimate=pl.CostEstimate(
            flops=6 * hidden * feats * steps * points, bytes_accessed=4 * 1024 * 1024, transcendentals=hidden * steps * points
        ),
    )(
        latent, jnp.transpose(targets, (1, 0, 2)), w1, jnp.transpose(w2), noise_table, member_ids,
        lat_weight[None, :], area_index[None, :], var_weight[None, :],
    )
    return jnp.reshape(loss, (1,)), latent_grad, w1_grad, jnp.transpose(w2_grad)


def solution(mesh):
    return jax.shard_map(
        on_device if tuple(mesh.shape[a] for a in ("grid", "member")) != (4, 4) else fused_on_device,
        mesh=mesh,
        in_specs=(
            P(None, "member", None, ("rep", "grid")),
            P(None, None, ("rep", "grid")),
            P("grid", None),
            P(None, "grid"),
            P(),
            P(("rep", "member")),
            P(),
            P(("rep", "grid")),
            P(),
        ),
        out_specs=(
            P("rep"),
            P(None, "member", None, ("rep", "grid")),
            P(("rep", "grid"), None),
            P(None, ("rep", "grid")),
        ),
        check_vma=False,
    )
```

```python
import functools
import math

import jax
import jax.numpy as jnp
from jax import lax
from jax.experimental import pallas as pl
from jax.experimental.pallas import tpu as pltpu
from jax.sharding import PartitionSpec as P

alpha_fair = 0.95
smooth_width = 0.05
loss_scale = 64.0
grad_shrink = 1.0 / 1024.0


def smooth_abs(diff):
    return jnp.sqrt(diff * diff + smooth_width * smooth_width) - smooth_width


def smooth_sign(diff):
    return diff / jnp.sqrt(diff * diff + smooth_width * smooth_width)


def on_device(latent, targets, w1, w2, noise_table, member_ids, lat_weight, area_index, var_weight):
    members = lax.axis_size("member")
    grid_count = lax.axis_size("grid")
    inputs = latent[:, 0]
    steps = inputs.shape[0]
    points = inputs.shape[2]
    variables = targets.shape[1]
    total_points = points * grid_count
    fairness = (1.0 - alpha_fair) / members
    pair_coef = (1.0 - fairness) / (members * (members - 1))
    lookup = (jnp.arange(lat_weight.shape[0])[:, None] == area_index[None, :]).astype(jnp.float32)
    area = jnp.sum(lookup * lat_weight[:, None], axis=0)
    local_area = jnp.sum(area)
    area_total = lax.psum(local_area, "grid")
    chooser = (jnp.arange(noise_table.shape[0]) == member_ids[0]).astype(jnp.float32)
    noise = jnp.sum(noise_table * chooser[:, None], axis=0)
    before = (
        jnp.einsum(
            "hl,slp->shp",
            lax.all_gather(w1, "grid", axis=0, tiled=True),
            inputs,
            preferred_element_type=jnp.float32,
        )
        + noise[None, :, None]
    )
    hidden = jax.nn.gelu(before).astype(jnp.bfloat16)
    w2_full = lax.all_gather(w2, "grid", axis=1, tiled=True)
    fields = jnp.einsum("vh,shp->svp", w2_full, hidden, preferred_element_type=jnp.float32)
    weight = var_weight[:, None] * area[None, :]
    everyone = lax.all_gather(fields[None], "member", axis=0, tiled=True)
    spread = fields[None] - everyone
    pair_loss = jnp.sum(smooth_abs(spread), axis=0)
    pair_grad = jnp.sum(smooth_sign(spread), axis=0)
    error = fields - targets
    term = smooth_abs(error) / members - 0.5 * pair_coef * pair_loss
    loss_local = jnp.sum(weight[None] * term)
    cotangent = (
        loss_scale * weight[None] * (smooth_sign(error) / members - pair_coef * pair_grad)
    ).astype(jnp.bfloat16)
    back_hidden = jnp.einsum("vh,svp->shp", w2_full, cotangent, preferred_element_type=jnp.float32)
    unused, pullback = jax.vjp(jax.nn.gelu, before)
    back_before = pullback(back_hidden)[0].astype(jnp.bfloat16)
    back_input = jnp.einsum(
        "hl,shp->slp",
        lax.all_gather(w1, "grid", axis=0, tiled=True),
        back_before,
        preferred_element_type=jnp.float32,
    )
    grad_first = jnp.einsum("shp,slp->hl", back_before, inputs, preferred_element_type=jnp.float32)
    grad_second = jnp.einsum("shp,svp->hv", hidden, cotangent, preferred_element_type=jnp.float32)
    grid_sums = (
        lax.psum_scatter(grad_first, "grid", scatter_dimension=0, tiled=True),
        lax.psum_scatter(grad_second, "grid", scatter_dimension=0, tiled=True),
    )
    first_rows, second_rows = lax.psum((grid_sums[0], grid_sums[1]), "member")
    loss_total = lax.psum(loss_local, ("grid", "member"))
    scale = total_points / area_total
    latent_grad = (back_input * scale).astype(jnp.bfloat16)[:, None]
    w1_grad = first_rows * (scale * grad_shrink)
    w2_grad = jnp.transpose(second_rows) * (scale * grad_shrink)
    loss = jnp.reshape(loss_total / (area_total * steps * variables), (1,))
    return (loss, latent_grad, w1_grad, w2_grad)


MESH = pl.DeviceIdType.MESH
GRID = 4
MEMB = 4
TANH_SCALE = math.sqrt(2.0 / math.pi)
CUBIC = 0.044715


def gelu_and_slope(x):
    square = x * x
    t = jnp.tanh(TANH_SCALE * x * (1.0 + CUBIC * square))
    half = 0.5 * (1.0 + t)
    slope = half + 0.5 * x * (1.0 - t * t) * (TANH_SCALE * (1.0 + 3.0 * CUBIC * square))
    return x * half, slope


def pick(index, values):
    result = values[-1]
    for i in range(len(values) - 1):
        result = jnp.where(index == i, values[i], result)
    return result


def dot(a, b, contract):
    return lax.dot_general(a, b, ((contract[:1], contract[1:]), ((), ())), preferred_element_type=jnp.float32)


class Slots:
    def __init__(self):
        self.count = 0

    def take(self, n=1):
        self.count += n
        return self.count - n


SEM = Slots()
AREA, W_Z = SEM.take(4), SEM.take(4)
W_PLANE, W_CORE = SEM.take(3 * 4), SEM.take(4 * 4)
F_CORE, F_X, F_DIAG = SEM.take(2), SEM.take(2), SEM.take(2)
G_CORE, G_X, G_Z = SEM.take(4), SEM.take(4), SEM.take(4)
G_ENDX, G_ENDC, G_ENDD = SEM.take(1), SEM.take(1), SEM.take(1)
L_MEM, L_GRID = SEM.take(4), SEM.take(4)
QUART = 4
EXTRA = 16


def fused(
    lat_hbm, tgt_hbm, w1_hbm, w2_ref, table_ref, ids_ref, latw_ref, aidx_ref, vw_ref,
    loss_ref, lg_ref, w1g_ref, w2g_ref,
    lat, tgt, wx, noise, slope, hid, fall, cot, bb, gbuf, acc, csend, crecv, xs, xr, zs, zr, fin, pad,
    abuf, lmem, lgrid, ss, rs, ls,
):
    y, g, m = lax.axis_index("rep"), lax.axis_index("grid"), lax.axis_index("member")
    c = lax.rem(m, 2)
    x = lax.div(m, 2)
    quarter = 2 * x + y
    core_peer, x_peer = m + 1 - 2 * c, lax.rem(m + 2, 4)
    diag_peer = lax.rem(core_peer + 2, 4)
    steps, _, feats, points = lat_hbm.shape
    variables = tgt_hbm.shape[0]
    rows = w1_hbm.shape[0]
    half = rows // 2
    span = feats // QUART
    fairness = (1.0 - alpha_fair) / MEMB
    pair_coef = (1.0 - fairness) / (MEMB * (MEMB - 1))

    def block(t):
        return pl.ds(pl.multiple_of(t * rows, rows), rows)

    def send(src, dst, s_index, r_index, **where):
        return pltpu.make_async_remote_copy(
            src_ref=src, dst_ref=dst, send_sem=ss.at[s_index], recv_sem=rs.at[r_index],
            device_id={"grid": where.get("grid", g), "member": where.get("member", m), "rep": where.get("rep", y)},
            device_id_type=MESH,
        )

    def first_rows(o):
        own = wx[pl.ds(o, 1)][0]
        return jnp.concatenate(
            [jnp.concatenate([own[q, i, :half] for q in range(QUART)], axis=1) for i in range(2)], axis=0
        )

    def second_columns(o):
        own = wx[pl.ds(o, 1)][0]
        return jnp.concatenate([own[q, i, half:] for q in range(QUART) for i in range(2)], axis=0)[:, :rows]

    w1_in = [
        pltpu.make_async_copy(
            w1_hbm.at[pl.ds(i * half, half), pl.ds(q * span, span)], wx.at[g, q, i, pl.ds(0, half)], ls.at[8 + 2 * q + i]
        )
        for q in range(QUART)
        for i in range(2)
    ]
    for copy in w1_in:
        copy.start()
    lat_in = pltpu.make_async_copy(lat_hbm.at[:, 0], lat, ls.at[1])
    lat_in.start()
    tgt_in = [pltpu.make_async_copy(tgt_hbm.at[:, s], tgt.at[s], ls.at[5 + s]) for s in range(steps)]
    for copy in tgt_in:
        copy.start()

    barrier = pltpu.get_barrier_semaphore()

    def greet(**where):
        pl.semaphore_signal(
            barrier, inc=1, device_id_type=MESH,
            device_id={"grid": where.get("grid", g), "member": where.get("member", m), "rep": where.get("rep", y)},
        )

    for k in range(1, 4):
        greet(grid=lax.rem(g + k, 4))
        greet(member=lax.rem(m + k, 4))
    greet(rep=1 - y)
    greet(rep=1 - y, member=x_peer)

    pad[...] = jnp.zeros_like(pad)
    pad[:rows, :variables] = w2_ref[...].astype(jnp.float32)
    second = jnp.transpose(pad[...]).astype(jnp.bfloat16)
    for q in range(QUART):
        for i in range(2):
            at = (2 * q + i) * EXTRA
            wx[pl.ds(g, 1), q, i, half:] = second[None, at : at + EXTRA]
    for copy in w1_in:
        copy.wait()
    pl.semaphore_wait(barrier, 8)

    piece = wx.at[g, quarter, c]
    w_sends = [send(piece, piece, W_Z + k, W_Z + g, grid=lax.rem(g + k, 4)) for k in range(1, 4)]
    for copy in w_sends:
        copy.start()

    n_lat = latw_ref.shape[1]
    diagonal = lax.broadcasted_iota(jnp.int32, (n_lat, n_lat), 0) == lax.broadcasted_iota(jnp.int32, (n_lat, n_lat), 1)
    lat_col = jnp.sum(jnp.where(diagonal, latw_ref[...], 0.0), axis=1, keepdims=True)
    lookup = lax.broadcasted_iota(jnp.int32, (n_lat, points), 0) == aidx_ref[...]
    area = jnp.sum(jnp.where(lookup, lat_col, 0.0), axis=0, keepdims=True)
    abuf[pl.ds(g, 1)] = jnp.full((1, 8, 128), jnp.sum(area), jnp.float32)
    area_sends = [
        send(abuf.at[g], abuf.at[g], AREA + k, AREA + g, grid=lax.rem(g + k, 4)) for k in range(1, 4)
    ]
    for copy in area_sends:
        copy.start()
    diagonal = lax.broadcasted_iota(jnp.int32, (variables, variables), 0) == lax.broadcasted_iota(jnp.int32, (variables, variables), 1)
    var_col = jnp.sum(jnp.where(diagonal, vw_ref[...], 0.0), axis=1, keepdims=True)
    weight = var_col * area

    chosen = lax.broadcasted_iota(jnp.int32, table_ref.shape, 0) == ids_ref[0]
    noise_row = jnp.sum(jnp.where(chosen, table_ref[...], 0.0), axis=0, keepdims=True)
    noise[...] = jnp.transpose(jnp.broadcast_to(noise_row, (128, noise_row.shape[1])))
    cot[...] = jnp.zeros_like(cot)
    lat_in.wait()

    fields = [None] * steps
    field_sends = []
    mirrored = g >= 2
    near = jnp.where(mirrored, 3 - g, g)
    owners = []
    for j in range(GRID):
        o = pick(near, (j, (1, 0, 2, 3)[j]))
        owners.append(jnp.where(mirrored, 3 - o, o))
    plane = ((dict(member=x_peer), 2 * (1 - x) + y), (dict(rep=1 - y), 2 * x + 1 - y),
             (dict(member=x_peer, rep=1 - y), 2 * (1 - x) + 1 - y))

    def spread_piece(o):
        mine = wx.at[o, quarter, c]
        send(mine, mine, W_Z + o, W_Z + o).wait_recv()
        for i, (where, _) in enumerate(plane):
            copy = send(mine, mine, W_PLANE + 4 * i + o, W_PLANE + 4 * i + o, **where)
            copy.start()
            w_sends.append(copy)
        copy = send(mine, mine, W_CORE + 12 + o, W_CORE + 12 + o, member=core_peer)
        copy.start()
        w_sends.append(copy)

    def pass_to_core(o):
        for i, (_, q) in enumerate(plane):
            got = wx.at[o, q, c]
            send(got, got, W_PLANE + 4 * i + o, W_PLANE + 4 * i + o).wait_recv()
            copy = send(got, got, W_CORE + 4 * i + o, W_CORE + 4 * i + o, member=core_peer)
            copy.start()
            w_sends.append(copy)

    def have_block(o):
        for i, q in enumerate([q for _, q in plane] + [quarter]):
            got = wx.at[o, q, 1 - c]
            send(got, got, W_CORE + 4 * i + o, W_CORE + 4 * i + o).wait_recv()

    for j in range(GRID):
        o = owners[j]
        if j == 1:
            for later in owners[1:]:
                spread_piece(later)
        if j > 0:
            for later in owners[1:3] if j == 1 else owners[j + 1 : j + 2]:
                pass_to_core(later)
            have_block(o)
        shift = noise[block(o), :]
        shift = jnp.concatenate([shift] * (points // 128), axis=1)
        own_first, own_second = first_rows(o), second_columns(o)
        for s in range(steps):
            before = dot(own_first, lat[s], (1, 0)) + shift
            value, grad = gelu_and_slope(before)
            value = value.astype(jnp.bfloat16)
            cols = slice(s * points, (s + 1) * points)
            slope[block(o), cols] = grad
            hid[block(o), cols] = value
            part = dot(own_second, value, (1, 0))
            fields[s] = part if j == 0 else fields[s] + part
            if j == GRID - 1:
                fall[pl.ds(m, 1), s] = fields[s][None, : fall.shape[2]]
                mine = fall.at[m, s]
                pair = (
                    send(mine, mine, F_X + s, F_X + s, member=x_peer),
                    send(mine, mine, F_CORE + s, F_CORE + s, member=core_peer),
                )
                for copy in pair:
                    copy.start()
                field_sends.extend(pair)

    for copy in tgt_in:
        copy.wait()
    for k in range(1, 4):
        o = lax.rem(g + k, 4)
        send(abuf.at[o], abuf.at[o], AREA + k, AREA + o).wait_recv()
    area_total = abuf[0] + abuf[1] + abuf[2] + abuf[3]
    area_total = area_total[:1, :1]
    scale = (points * GRID) / area_total

    def relay(s):
        theirs = fall.at[x_peer, s]
        send(theirs, theirs, F_X + s, F_X + s).wait_recv()
        onward = send(theirs, theirs, F_DIAG + s, F_DIAG + s, member=core_peer)
        onward.start()
        field_sends.append(onward)

    def against_target(s):
        error = fields[s][:variables] - tgt[s]
        root = jnp.sqrt(error * error + smooth_width * smooth_width)
        return (root - smooth_width) / MEMB, error / root / MEMB

    def against(s, peer, term, grad):
        spread = fields[s][:variables] - fall[pl.ds(peer, 1), s][0, :variables]
        root = jnp.sqrt(spread * spread + smooth_width * smooth_width)
        return term - (0.5 * pair_coef) * (root - smooth_width), grad - pair_coef * (spread / root)

    def arrived(s, peer, index):
        ref = fall.at[peer, s]
        send(ref, ref, index + s, index + s).wait_recv()

    losses = []

    def backward(s, term, grad):
        losses.append(jnp.sum(weight * term))
        cols = slice(s * points, (s + 1) * points)
        cot[:variables, cols] = (loss_scale * weight * grad).astype(jnp.bfloat16)
        for o in range(GRID):
            hidden_rows = slice(o * rows, (o + 1) * rows)
            back = dot(second_columns(o), cot[:, cols], (0, 0))
            bb[hidden_rows, cols] = (back * slope[hidden_rows, cols]).astype(jnp.bfloat16)

    state = []
    for s in range(steps):
        term, grad = against_target(s)
        arrived(s, core_peer, F_CORE)
        term, grad = against(s, core_peer, term, grad)
        relay(s)
        state.append(against(s, x_peer, term, grad))
        if s > 0:
            arrived(s - 1, diag_peer, F_DIAG)
            backward(s - 1, *against(s - 1, diag_peer, *state[s - 1]))
    arrived(steps - 1, diag_peer, F_DIAG)
    backward(steps - 1, *against(steps - 1, diag_peer, *state[-1]))
    loss_sum = sum(losses[1:], losses[0])

    lmem[pl.ds(m, 1)] = jnp.full((1, 8, 128), loss_sum, jnp.float32)
    late = [send(lmem.at[m], lmem.at[m], L_MEM + k, L_MEM + m, member=lax.rem(m + k, 4)) for k in range(1, 4)]
    for copy in late:
        copy.start()

    order = [
        pick(g, (3, 3, 0, 0)),
        pick(g, (2, 0, 3, 1)),
        pick(g, (1, 2, 1, 2)),
        g,
    ]
    fourth = half // 2
    my_half = pl.ds(pl.multiple_of(c * half, half), half)
    their_half = pl.ds(pl.multiple_of((1 - c) * half, half), half)
    my_fourth = pl.ds(pl.multiple_of(x * fourth, fourth), fourth)
    their_fourth = pl.ds(pl.multiple_of((1 - x) * fourth, fourth), fourth)

    def start(copy):
        copy.start()
        late.append(copy)

    def partial(j):
        t = order[j]
        first = dot(bb[block(t), :points], lat[0], (1, 1))
        for s in range(1, steps):
            first = first + dot(bb[block(t), s * points : (s + 1) * points], lat[s], (1, 1))
        gbuf[j, :, :feats] = first
        gbuf[j, :, feats:] = dot(hid[block(t), :], cot[...], (1, 1))
        csend[j] = gbuf[j, their_half].astype(jnp.bfloat16)
        start(send(csend.at[j], crecv.at[j], G_CORE + j, G_CORE + j, member=core_peer))

    def over_x(j):
        send(csend.at[j], crecv.at[j], G_CORE + j, G_CORE + j).wait_recv()
        acc[...] = gbuf[j, my_half] + crecv[j].astype(jnp.float32)
        xs[j] = acc[their_fourth].astype(jnp.bfloat16)
        gbuf[j, :fourth] = acc[my_fourth]
        start(send(xs.at[j], xr.at[j], G_X + j, G_X + j, member=x_peer))

    def along_z(j):
        send(xs.at[j], xr.at[j], G_X + j, G_X + j).wait_recv()
        total = gbuf[j, :fourth] + xr[j].astype(jnp.float32)
        if j == GRID - 1:
            gbuf[j, :fourth] = total
        else:
            zs[j] = total.astype(jnp.bfloat16)
            start(send(zs.at[j], zr.at[g], G_Z + j, G_Z + g, grid=order[j]))

    def back_input(s, q):
        cols = slice(s * points, (s + 1) * points)
        left = jnp.concatenate([wx[o, q, i, :half] for o in range(GRID) for i in range(2)], axis=0)
        lg_ref[s, 0, q * span : (q + 1) * span] = (dot(left, bb[:, cols], (0, 0)) * scale).astype(jnp.bfloat16)

    pieces = [(s, q) for s in range(steps) for q in range(QUART)]
    for i in range(GRID + 1):
        if i < GRID:
            partial(i)
        if i > 0:
            over_x(i - 1)
    back_input(*pieces[0])
    back_input(*pieces[1])
    for j in range(GRID):
        along_z(j)
        if j == 0:
            for k in range(1, 4):
                o = lax.rem(m + k, 4)
                send(lmem.at[o], lmem.at[o], L_MEM + k, L_MEM + o).wait_recv()
            lgrid[pl.ds(g, 1)] = (lmem[0] + lmem[1] + lmem[2] + lmem[3])[None]
            for k in range(1, 4):
                start(send(lgrid.at[g], lgrid.at[g], L_GRID + k, L_GRID + g, grid=lax.rem(g + k, 4)))
        for s, q in pieces[2 + 2 * j : 4 + 2 * j] if j < 3 else []:
            back_input(s, q)
    for k in range(1, 4):
        o = lax.rem(g + k, 4)
        send(lgrid.at[o], lgrid.at[o], L_GRID + k, L_GRID + o).wait_recv()
    loss_total = lgrid[0] + lgrid[1] + lgrid[2] + lgrid[3]
    loss_ref[...] = loss_total[:1, :1] / (area_total * (steps * variables))

    total = gbuf[GRID - 1, :fourth]
    for k in range(1, 4):
        o = lax.rem(g + k, 4)
        send(zr.at[o], zr.at[o], G_Z + k, G_Z + o).wait_recv()
        total = total + zr[pl.ds(o, 1)][0].astype(jnp.float32)
    fin[pl.ds(m, 1)] = (total * (scale * grad_shrink)).astype(jnp.bfloat16)[None]

    def give(o, s_index, peer):
        start(send(fin.at[o], fin.at[o], s_index, s_index, member=peer))

    def got(o, s_index):
        send(fin.at[o], fin.at[o], s_index, s_index).wait_recv()

    def finish(o):
        place = 2 * lax.rem(o, 2) + lax.div(o, 2)
        here = pl.ds(pl.multiple_of(place * fourth, fourth), fourth)
        value = fin[pl.ds(o, 1)][0].astype(jnp.float32)
        w1g_ref[here] = value[:, :feats]
        w2g_ref[here] = value[:, feats : feats + variables]

    give(m, G_ENDX, x_peer)
    give(m, G_ENDC, core_peer)
    finish(m)
    got(core_peer, G_ENDC)
    finish(core_peer)
    got(x_peer, G_ENDX)
    give(x_peer, G_ENDD, core_peer)
    finish(x_peer)
    got(diag_peer, G_ENDD)
    finish(diag_peer)

    for copy in w_sends + area_sends + field_sends + late:
        copy.wait_send()


def fused_on_device(latent, targets, w1, w2, noise_table, member_ids, lat_weight, area_index, var_weight):
    steps, _, feats, points = latent.shape
    variables = targets.shape[1]
    rows = w1.shape[0]
    hidden = rows * GRID
    half = rows // 2
    wide = feats + 128
    fourth = half // 2
    padded = -(-variables // 8) * 8
    f32, bf16 = jnp.float32, jnp.bfloat16
    hbm, vmem = pl.BlockSpec(memory_space=pltpu.HBM), pl.BlockSpec(memory_space=pltpu.VMEM)
    smem = pl.BlockSpec(memory_space=pltpu.SMEM)
    loss, latent_grad, w1_grad, w2_grad = pl.pallas_call(
        fused,
        out_shape=(
            jax.ShapeDtypeStruct((1, 1), f32),
            pltpu.VMEM(latent.shape, bf16),
            pltpu.VMEM((rows, feats), f32),
            pltpu.VMEM((rows, variables), f32),
        ),
        in_specs=[hbm, hbm, hbm, vmem, vmem, smem, vmem, vmem, vmem],
        out_specs=(vmem, vmem, vmem, vmem),
        scratch_shapes=[
            pltpu.VMEM((steps, feats, points), bf16),
            pltpu.VMEM((steps, variables, points), f32),
            pltpu.VMEM((GRID, QUART, 2, half + EXTRA, feats // QUART), bf16),
            pltpu.VMEM((hidden, 128), f32),
            pltpu.VMEM((hidden, steps * points), f32),
            pltpu.VMEM((hidden, steps * points), bf16),
            pltpu.VMEM((MEMB, steps, padded, points), f32),
            pltpu.VMEM((128, steps * points), bf16),
            pltpu.VMEM((hidden, steps * points), bf16),
            pltpu.VMEM((GRID, rows, wide), f32),
            pltpu.VMEM((half, wide), f32),
            pltpu.VMEM((GRID, half, wide), bf16),
            pltpu.VMEM((GRID, half, wide), bf16),
            pltpu.VMEM((GRID, fourth, wide), bf16),
            pltpu.VMEM((GRID, fourth, wide), bf16),
            pltpu.VMEM((GRID - 1, fourth, wide), bf16),
            pltpu.VMEM((GRID, fourth, wide), bf16),
            pltpu.VMEM((MEMB, fourth, wide), bf16),
            pltpu.VMEM((256, 128), f32),
            pltpu.VMEM((GRID, 8, 128), f32),
            pltpu.VMEM((MEMB, 8, 128), f32),
            pltpu.VMEM((GRID, 8, 128), f32),
            pltpu.SemaphoreType.DMA((SEM.count,)),
            pltpu.SemaphoreType.DMA((SEM.count,)),
            pltpu.SemaphoreType.DMA((16,)),
        ],
        compiler_params=pltpu.CompilerParams(
            collective_id=0, has_side_effects=True, vmem_limit_bytes=60 * 1024 * 1024
        ),
        cost_estimate=pl.CostEstimate(
            flops=6 * hidden * feats * steps * points, bytes_accessed=4 * 1024 * 1024, transcendentals=hidden * steps * points
        ),
    )(
        latent, jnp.transpose(targets, (1, 0, 2)), w1, jnp.transpose(w2), noise_table, member_ids,
        lat_weight[None, :], area_index[None, :], var_weight[None, :],
    )
    return jnp.reshape(loss, (1,)), latent_grad, w1_grad, jnp.transpose(w2_grad)


def solution(mesh):
    return jax.shard_map(
        on_device if tuple(mesh.shape[a] for a in ("grid", "member")) != (4, 4) else fused_on_device,
        mesh=mesh,
        in_specs=(
            P(None, "member", None, ("rep", "grid")),
            P(None, None, ("rep", "grid")),
            P("grid", None),
            P(None, "grid"),
            P(),
            P(("rep", "member")),
            P(),
            P(("rep", "grid")),
            P(),
        ),
        out_specs=(
            P("rep"),
            P(None, "member", None, ("rep", "grid")),
            P(("rep", "grid"), None),
            P(None, ("rep", "grid")),
        ),
        check_vma=False,
    )
```

```python
import functools
import math

import jax
import jax.numpy as jnp
from jax import lax
from jax.experimental import pallas as pl
from jax.experimental.pallas import tpu as pltpu
from jax.sharding import PartitionSpec as P

alpha_fair = 0.95
smooth_width = 0.05
loss_scale = 64.0
grad_shrink = 1.0 / 1024.0


def smooth_abs(diff):
    return jnp.sqrt(diff * diff + smooth_width * smooth_width) - smooth_width


def smooth_sign(diff):
    return diff / jnp.sqrt(diff * diff + smooth_width * smooth_width)


def on_device(latent, targets, w1, w2, noise_table, member_ids, lat_weight, area_index, var_weight):
    members = lax.axis_size("member")
    grid_count = lax.axis_size("grid")
    inputs = latent[:, 0]
    steps = inputs.shape[0]
    points = inputs.shape[2]
    variables = targets.shape[1]
    total_points = points * grid_count
    fairness = (1.0 - alpha_fair) / members
    pair_coef = (1.0 - fairness) / (members * (members - 1))
    lookup = (jnp.arange(lat_weight.shape[0])[:, None] == area_index[None, :]).astype(jnp.float32)
    area = jnp.sum(lookup * lat_weight[:, None], axis=0)
    local_area = jnp.sum(area)
    area_total = lax.psum(local_area, "grid")
    chooser = (jnp.arange(noise_table.shape[0]) == member_ids[0]).astype(jnp.float32)
    noise = jnp.sum(noise_table * chooser[:, None], axis=0)
    before = (
        jnp.einsum(
            "hl,slp->shp",
            lax.all_gather(w1, "grid", axis=0, tiled=True),
            inputs,
            preferred_element_type=jnp.float32,
        )
        + noise[None, :, None]
    )
    hidden = jax.nn.gelu(before).astype(jnp.bfloat16)
    w2_full = lax.all_gather(w2, "grid", axis=1, tiled=True)
    fields = jnp.einsum("vh,shp->svp", w2_full, hidden, preferred_element_type=jnp.float32)
    weight = var_weight[:, None] * area[None, :]
    everyone = lax.all_gather(fields[None], "member", axis=0, tiled=True)
    spread = fields[None] - everyone
    pair_loss = jnp.sum(smooth_abs(spread), axis=0)
    pair_grad = jnp.sum(smooth_sign(spread), axis=0)
    error = fields - targets
    term = smooth_abs(error) / members - 0.5 * pair_coef * pair_loss
    loss_local = jnp.sum(weight[None] * term)
    cotangent = (
        loss_scale * weight[None] * (smooth_sign(error) / members - pair_coef * pair_grad)
    ).astype(jnp.bfloat16)
    back_hidden = jnp.einsum("vh,svp->shp", w2_full, cotangent, preferred_element_type=jnp.float32)
    unused, pullback = jax.vjp(jax.nn.gelu, before)
    back_before = pullback(back_hidden)[0].astype(jnp.bfloat16)
    back_input = jnp.einsum(
        "hl,shp->slp",
        lax.all_gather(w1, "grid", axis=0, tiled=True),
        back_before,
        preferred_element_type=jnp.float32,
    )
    grad_first = jnp.einsum("shp,slp->hl", back_before, inputs, preferred_element_type=jnp.float32)
    grad_second = jnp.einsum("shp,svp->hv", hidden, cotangent, preferred_element_type=jnp.float32)
    grid_sums = (
        lax.psum_scatter(grad_first, "grid", scatter_dimension=0, tiled=True),
        lax.psum_scatter(grad_second, "grid", scatter_dimension=0, tiled=True),
    )
    first_rows, second_rows = lax.psum((grid_sums[0], grid_sums[1]), "member")
    loss_total = lax.psum(loss_local, ("grid", "member"))
    scale = total_points / area_total
    latent_grad = (back_input * scale).astype(jnp.bfloat16)[:, None]
    w1_grad = first_rows * (scale * grad_shrink)
    w2_grad = jnp.transpose(second_rows) * (scale * grad_shrink)
    loss = jnp.reshape(loss_total / (area_total * steps * variables), (1,))
    return (loss, latent_grad, w1_grad, w2_grad)


MESH = pl.DeviceIdType.MESH
GRID = 4
MEMB = 4
TANH_SCALE = math.sqrt(2.0 / math.pi)
CUBIC = 0.044715


def gelu_and_slope(x):
    square = x * x
    t = jnp.tanh(TANH_SCALE * x * (1.0 + CUBIC * square))
    half = 0.5 * (1.0 + t)
    slope = half + 0.5 * x * (1.0 - t * t) * (TANH_SCALE * (1.0 + 3.0 * CUBIC * square))
    return x * half, slope


def pick(index, values):
    result = values[-1]
    for i in range(len(values) - 1):
        result = jnp.where(index == i, values[i], result)
    return result


def dot(a, b, contract):
    return lax.dot_general(a, b, ((contract[:1], contract[1:]), ((), ())), preferred_element_type=jnp.float32)


class Slots:
    def __init__(self):
        self.count = 0

    def take(self, n=1):
        self.count += n
        return self.count - n


SEM = Slots()
AREA, W_Z = SEM.take(4), SEM.take(4)
W_PLANE, W_CORE = SEM.take(3 * 4), SEM.take(4 * 4)
F_CORE, F_X, F_DIAG = SEM.take(2), SEM.take(2), SEM.take(2)
G_CORE, G_X, G_Z = SEM.take(4), SEM.take(4), SEM.take(4)
G_ENDX, G_ENDC, G_ENDD = SEM.take(1), SEM.take(1), SEM.take(1)
L_MEM, L_GRID = SEM.take(4), SEM.take(4)
QUART = 4
EXTRA = 16


def fused(
    lat_hbm, tgt_hbm, w1_hbm, w2_ref, table_ref, ids_ref, latw_ref, aidx_ref, vw_ref,
    loss_ref, lg_ref, w1g_ref, w2g_ref,
    lat, tgt, wx, noise, slope, hid, fall, cot, bb, gbuf, acc, csend, crecv, xs, xr, zs, zr, fin, pad,
    abuf, lmem, lgrid, ss, rs, ls,
):
    y, g, m = lax.axis_index("rep"), lax.axis_index("grid"), lax.axis_index("member")
    c = lax.rem(m, 2)
    x = lax.div(m, 2)
    quarter = 2 * x + y
    core_peer, x_peer = m + 1 - 2 * c, lax.rem(m + 2, 4)
    diag_peer = lax.rem(core_peer + 2, 4)
    steps, _, feats, points = lat_hbm.shape
    variables = tgt_hbm.shape[0]
    rows = w1_hbm.shape[0]
    half = rows // 2
    span = feats // QUART
    fairness = (1.0 - alpha_fair) / MEMB
    pair_coef = (1.0 - fairness) / (MEMB * (MEMB - 1))

    def block(t):
        return pl.ds(pl.multiple_of(t * rows, rows), rows)

    def send(src, dst, s_index, r_index, **where):
        return pltpu.make_async_remote_copy(
            src_ref=src, dst_ref=dst, send_sem=ss.at[s_index], recv_sem=rs.at[r_index],
            device_id={"grid": where.get("grid", g), "member": where.get("member", m), "rep": where.get("rep", y)},
            device_id_type=MESH,
        )

    def first_rows(o):
        own = wx[pl.ds(o, 1)][0]
        return jnp.concatenate(
            [jnp.concatenate([own[q, i, :half] for q in range(QUART)], axis=1) for i in range(2)], axis=0
        )

    def second_columns(o):
        own = wx[pl.ds(o, 1)][0]
        return jnp.concatenate([own[q, i, half:] for q in range(QUART) for i in range(2)], axis=0)[:, :rows]

    w1_in = [
        pltpu.make_async_copy(
            w1_hbm.at[pl.ds(i * half, half), pl.ds(q * span, span)], wx.at[g, q, i, pl.ds(0, half)], ls.at[8 + 2 * q + i]
        )
        for q in range(QUART)
        for i in range(2)
    ]
    for copy in w1_in:
        copy.start()
    lat_in = pltpu.make_async_copy(lat_hbm.at[:, 0], lat, ls.at[1])
    lat_in.start()
    tgt_in = [pltpu.make_async_copy(tgt_hbm.at[:, s], tgt.at[s], ls.at[5 + s]) for s in range(steps)]
    for copy in tgt_in:
        copy.start()

    barrier = pltpu.get_barrier_semaphore()

    def greet(**where):
        pl.semaphore_signal(
            barrier, inc=1, device_id_type=MESH,
            device_id={"grid": where.get("grid", g), "member": where.get("member", m), "rep": where.get("rep", y)},
        )

    for k in range(1, 4):
        greet(grid=lax.rem(g + k, 4))
        greet(member=lax.rem(m + k, 4))
    greet(rep=1 - y)
    greet(rep=1 - y, member=x_peer)

    pad[...] = jnp.zeros_like(pad)
    pad[:rows, :variables] = w2_ref[...].astype(jnp.float32)
    second = jnp.transpose(pad[...]).astype(jnp.bfloat16)
    for q in range(QUART):
        for i in range(2):
            at = (2 * q + i) * EXTRA
            wx[pl.ds(g, 1), q, i, half:] = second[None, at : at + EXTRA]
    for copy in w1_in:
        copy.wait()
    pl.semaphore_wait(barrier, 8)

    piece = wx.at[g, quarter, c]
    w_sends = [send(piece, piece, W_Z + k, W_Z + g, grid=lax.rem(g + k, 4)) for k in range(1, 4)]
    for copy in w_sends:
        copy.start()

    n_lat = latw_ref.shape[1]
    diagonal = lax.broadcasted_iota(jnp.int32, (n_lat, n_lat), 0) == lax.broadcasted_iota(jnp.int32, (n_lat, n_lat), 1)
    lat_col = jnp.sum(jnp.where(diagonal, latw_ref[...], 0.0), axis=1, keepdims=True)
    lookup = lax.broadcasted_iota(jnp.int32, (n_lat, points), 0) == aidx_ref[...]
    area = jnp.sum(jnp.where(lookup, lat_col, 0.0), axis=0, keepdims=True)
    abuf[pl.ds(g, 1)] = jnp.full((1, 8, 128), jnp.sum(area), jnp.float32)
    area_sends = [
        send(abuf.at[g], abuf.at[g], AREA + k, AREA + g, grid=lax.rem(g + k, 4)) for k in range(1, 4)
    ]
    for copy in area_sends:
        copy.start()
    diagonal = lax.broadcasted_iota(jnp.int32, (variables, variables), 0) == lax.broadcasted_iota(jnp.int32, (variables, variables), 1)
    var_col = jnp.sum(jnp.where(diagonal, vw_ref[...], 0.0), axis=1, keepdims=True)
    weight = var_col * area

    chosen = lax.broadcasted_iota(jnp.int32, table_ref.shape, 0) == ids_ref[0]
    noise_row = jnp.sum(jnp.where(chosen, table_ref[...], 0.0), axis=0, keepdims=True)
    noise[...] = jnp.transpose(jnp.broadcast_to(noise_row, (128, noise_row.shape[1])))
    cot[...] = jnp.zeros_like(cot)
    lat_in.wait()

    fields = [None] * steps
    field_sends = []
    mirrored = g >= 2
    near = jnp.where(mirrored, 3 - g, g)
    owners = []
    for j in range(GRID):
        o = pick(near, (j, (1, 0, 2, 3)[j]))
        owners.append(jnp.where(mirrored, 3 - o, o))
    plane = ((dict(member=x_peer), 2 * (1 - x) + y), (dict(rep=1 - y), 2 * x + 1 - y),
             (dict(member=x_peer, rep=1 - y), 2 * (1 - x) + 1 - y))

    def spread_piece(o):
        mine = wx.at[o, quarter, c]
        send(mine, mine, W_Z + o, W_Z + o).wait_recv()
        for i, (where, _) in enumerate(plane):
            copy = send(mine, mine, W_PLANE + 4 * i + o, W_PLANE + 4 * i + o, **where)
            copy.start()
            w_sends.append(copy)
        copy = send(mine, mine, W_CORE + 12 + o, W_CORE + 12 + o, member=core_peer)
        copy.start()
        w_sends.append(copy)

    def pass_to_core(o):
        for i, (_, q) in enumerate(plane):
            got = wx.at[o, q, c]
            send(got, got, W_PLANE + 4 * i + o, W_PLANE + 4 * i + o).wait_recv()
            copy = send(got, got, W_CORE + 4 * i + o, W_CORE + 4 * i + o, member=core_peer)
            copy.start()
            w_sends.append(copy)

    def have_block(o):
        for i, q in enumerate([q for _, q in plane] + [quarter]):
            got = wx.at[o, q, 1 - c]
            send(got, got, W_CORE + 4 * i + o, W_CORE + 4 * i + o).wait_recv()

    for j in range(GRID):
        o = owners[j]
        if j == 1:
            for later in owners[1:]:
                spread_piece(later)
        if j > 0:
            for later in owners[1:3] if j == 1 else owners[j + 1 : j + 2]:
                pass_to_core(later)
            have_block(o)
        shift = noise[block(o), :]
        shift = jnp.concatenate([shift] * (points // 128), axis=1)
        own_first, own_second = first_rows(o), second_columns(o)
        for s in range(steps):
            before = dot(own_first, lat[s], (1, 0)) + shift
            value, grad = gelu_and_slope(before)
            value = value.astype(jnp.bfloat16)
            cols = slice(s * points, (s + 1) * points)
            slope[block(o), cols] = grad
            hid[block(o), cols] = value
            part = dot(own_second, value, (1, 0))
            fields[s] = part if j == 0 else fields[s] + part
            if j == GRID - 1:
                fall[pl.ds(m, 1), s] = fields[s][None, : fall.shape[2]]
                mine = fall.at[m, s]
                pair = (
                    send(mine, mine, F_X + s, F_X + s, member=x_peer),
                    send(mine, mine, F_CORE + s, F_CORE + s, member=core_peer),
                )
                for copy in pair:
                    copy.start()
                field_sends.extend(pair)

    for copy in tgt_in:
        copy.wait()
    for k in range(1, 4):
        o = lax.rem(g + k, 4)
        send(abuf.at[o], abuf.at[o], AREA + k, AREA + o).wait_recv()
    area_total = abuf[0] + abuf[1] + abuf[2] + abuf[3]
    area_total = area_total[:1, :1]
    scale = (points * GRID) / area_total

    def relay(s):
        theirs = fall.at[x_peer, s]
        send(theirs, theirs, F_X + s, F_X + s).wait_recv()
        onward = send(theirs, theirs, F_DIAG + s, F_DIAG + s, member=core_peer)
        onward.start()
        field_sends.append(onward)

    def against_target(s):
        error = fields[s][:variables] - tgt[s]
        square = error * error + smooth_width * smooth_width
        inverse = lax.rsqrt(square)
        return (square * inverse - smooth_width) * (1.0 / MEMB), error * inverse * (1.0 / MEMB)

    def against(s, peer, term, grad):
        spread = fields[s][:variables] - fall[pl.ds(peer, 1), s][0, :variables]
        square = spread * spread + smooth_width * smooth_width
        inverse = lax.rsqrt(square)
        return (
            term - (0.5 * pair_coef) * (square * inverse - smooth_width),
            grad - pair_coef * (spread * inverse),
        )

    def arrived(s, peer, index):
        ref = fall.at[peer, s]
        send(ref, ref, index + s, index + s).wait_recv()

    losses = []

    def backward(s, term, grad):
        losses.append(jnp.sum(weight * term))
        cols = slice(s * points, (s + 1) * points)
        cot[:variables, cols] = (loss_scale * weight * grad).astype(jnp.bfloat16)
        for o in range(GRID):
            hidden_rows = slice(o * rows, (o + 1) * rows)
            back = dot(second_columns(o), cot[:, cols], (0, 0))
            bb[hidden_rows, cols] = (back * slope[hidden_rows, cols]).astype(jnp.bfloat16)

    state = []
    for s in range(steps):
        term, grad = against_target(s)
        arrived(s, core_peer, F_CORE)
        term, grad = against(s, core_peer, term, grad)
        relay(s)
        state.append(against(s, x_peer, term, grad))
        if s > 0:
            arrived(s - 1, diag_peer, F_DIAG)
            backward(s - 1, *against(s - 1, diag_peer, *state[s - 1]))
    arrived(steps - 1, diag_peer, F_DIAG)
    backward(steps - 1, *against(steps - 1, diag_peer, *state[-1]))
    loss_sum = sum(losses[1:], losses[0])

    lmem[pl.ds(m, 1)] = jnp.full((1, 8, 128), loss_sum, jnp.float32)
    late = [send(lmem.at[m], lmem.at[m], L_MEM + k, L_MEM + m, member=lax.rem(m + k, 4)) for k in range(1, 4)]
    for copy in late:
        copy.start()

    order = [
        pick(g, (3, 3, 0, 0)),
        pick(g, (2, 0, 3, 1)),
        pick(g, (1, 2, 1, 2)),
        g,
    ]
    fourth = half // 2
    my_half = pl.ds(pl.multiple_of(c * half, half), half)
    their_half = pl.ds(pl.multiple_of((1 - c) * half, half), half)
    my_fourth = pl.ds(pl.multiple_of(x * fourth, fourth), fourth)
    their_fourth = pl.ds(pl.multiple_of((1 - x) * fourth, fourth), fourth)

    def start(copy):
        copy.start()
        late.append(copy)

    def partial(j):
        t = order[j]
        first = dot(bb[block(t), :points], lat[0], (1, 1))
        for s in range(1, steps):
            first = first + dot(bb[block(t), s * points : (s + 1) * points], lat[s], (1, 1))
        gbuf[j, :, :feats] = first
        gbuf[j, :, feats:] = dot(hid[block(t), :], cot[...], (1, 1))
        csend[j] = gbuf[j, their_half].astype(jnp.bfloat16)
        start(send(csend.at[j], crecv.at[j], G_CORE + j, G_CORE + j, member=core_peer))

    def over_x(j):
        send(csend.at[j], crecv.at[j], G_CORE + j, G_CORE + j).wait_recv()
        acc[...] = gbuf[j, my_half] + crecv[j].astype(jnp.float32)
        xs[j] = acc[their_fourth].astype(jnp.bfloat16)
        gbuf[j, :fourth] = acc[my_fourth]
        start(send(xs.at[j], xr.at[j], G_X + j, G_X + j, member=x_peer))

    def along_z(j):
        send(xs.at[j], xr.at[j], G_X + j, G_X + j).wait_recv()
        total = gbuf[j, :fourth] + xr[j].astype(jnp.float32)
        if j == GRID - 1:
            gbuf[j, :fourth] = total
        else:
            zs[j] = total.astype(jnp.bfloat16)
            start(send(zs.at[j], zr.at[g], G_Z + j, G_Z + g, grid=order[j]))

    def back_input(s, q):
        cols = slice(s * points, (s + 1) * points)
        left = jnp.concatenate([wx[o, q, i, :half] for o in range(GRID) for i in range(2)], axis=0)
        lg_ref[s, 0, q * span : (q + 1) * span] = (dot(left, bb[:, cols], (0, 0)) * scale).astype(jnp.bfloat16)

    pieces = [(s, q) for s in range(steps) for q in range(QUART)]
    for i in range(GRID + 1):
        if i < GRID:
            partial(i)
        if i > 0:
            over_x(i - 1)
    back_input(*pieces[0])
    back_input(*pieces[1])
    for j in range(GRID):
        along_z(j)
        if j == 0:
            for k in range(1, 4):
                o = lax.rem(m + k, 4)
                send(lmem.at[o], lmem.at[o], L_MEM + k, L_MEM + o).wait_recv()
            lgrid[pl.ds(g, 1)] = (lmem[0] + lmem[1] + lmem[2] + lmem[3])[None]
            for k in range(1, 4):
                start(send(lgrid.at[g], lgrid.at[g], L_GRID + k, L_GRID + g, grid=lax.rem(g + k, 4)))
        for s, q in pieces[2 + 2 * j : 4 + 2 * j] if j < 3 else []:
            back_input(s, q)
    for k in range(1, 4):
        o = lax.rem(g + k, 4)
        send(lgrid.at[o], lgrid.at[o], L_GRID + k, L_GRID + o).wait_recv()
    loss_total = lgrid[0] + lgrid[1] + lgrid[2] + lgrid[3]
    loss_ref[...] = loss_total[:1, :1] / (area_total * (steps * variables))

    total = gbuf[GRID - 1, :fourth]
    for k in range(1, 4):
        o = lax.rem(g + k, 4)
        send(zr.at[o], zr.at[o], G_Z + k, G_Z + o).wait_recv()
        total = total + zr[pl.ds(o, 1)][0].astype(jnp.float32)
    fin[pl.ds(m, 1)] = (total * (scale * grad_shrink)).astype(jnp.bfloat16)[None]

    def give(o, s_index, peer):
        start(send(fin.at[o], fin.at[o], s_index, s_index, member=peer))

    def got(o, s_index):
        send(fin.at[o], fin.at[o], s_index, s_index).wait_recv()

    def finish(o):
        place = 2 * lax.rem(o, 2) + lax.div(o, 2)
        here = pl.ds(pl.multiple_of(place * fourth, fourth), fourth)
        value = fin[pl.ds(o, 1)][0].astype(jnp.float32)
        w1g_ref[here] = value[:, :feats]
        w2g_ref[here] = value[:, feats : feats + variables]

    give(m, G_ENDX, x_peer)
    give(m, G_ENDC, core_peer)
    finish(m)
    got(core_peer, G_ENDC)
    finish(core_peer)
    got(x_peer, G_ENDX)
    give(x_peer, G_ENDD, core_peer)
    finish(x_peer)
    got(diag_peer, G_ENDD)
    finish(diag_peer)

    for copy in w_sends + area_sends + field_sends + late:
        copy.wait_send()


def fused_on_device(latent, targets, w1, w2, noise_table, member_ids, lat_weight, area_index, var_weight):
    steps, _, feats, points = latent.shape
    variables = targets.shape[1]
    rows = w1.shape[0]
    hidden = rows * GRID
    half = rows // 2
    wide = feats + 128
    fourth = half // 2
    padded = -(-variables // 8) * 8
    f32, bf16 = jnp.float32, jnp.bfloat16
    hbm, vmem = pl.BlockSpec(memory_space=pltpu.HBM), pl.BlockSpec(memory_space=pltpu.VMEM)
    smem = pl.BlockSpec(memory_space=pltpu.SMEM)
    loss, latent_grad, w1_grad, w2_grad = pl.pallas_call(
        fused,
        out_shape=(
            jax.ShapeDtypeStruct((1, 1), f32),
            pltpu.VMEM(latent.shape, bf16),
            pltpu.VMEM((rows, feats), f32),
            pltpu.VMEM((rows, variables), f32),
        ),
        in_specs=[hbm, hbm, hbm, vmem, vmem, smem, vmem, vmem, vmem],
        out_specs=(vmem, vmem, vmem, vmem),
        scratch_shapes=[
            pltpu.VMEM((steps, feats, points), bf16),
            pltpu.VMEM((steps, variables, points), f32),
            pltpu.VMEM((GRID, QUART, 2, half + EXTRA, feats // QUART), bf16),
            pltpu.VMEM((hidden, 128), f32),
            pltpu.VMEM((hidden, steps * points), f32),
            pltpu.VMEM((hidden, steps * points), bf16),
            pltpu.VMEM((MEMB, steps, padded, points), f32),
            pltpu.VMEM((128, steps * points), bf16),
            pltpu.VMEM((hidden, steps * points), bf16),
            pltpu.VMEM((GRID, rows, wide), f32),
            pltpu.VMEM((half, wide), f32),
            pltpu.VMEM((GRID, half, wide), bf16),
            pltpu.VMEM((GRID, half, wide), bf16),
            pltpu.VMEM((GRID, fourth, wide), bf16),
            pltpu.VMEM((GRID, fourth, wide), bf16),
            pltpu.VMEM((GRID - 1, fourth, wide), bf16),
            pltpu.VMEM((GRID, fourth, wide), bf16),
            pltpu.VMEM((MEMB, fourth, wide), bf16),
            pltpu.VMEM((256, 128), f32),
            pltpu.VMEM((GRID, 8, 128), f32),
            pltpu.VMEM((MEMB, 8, 128), f32),
            pltpu.VMEM((GRID, 8, 128), f32),
            pltpu.SemaphoreType.DMA((SEM.count,)),
            pltpu.SemaphoreType.DMA((SEM.count,)),
            pltpu.SemaphoreType.DMA((16,)),
        ],
        compiler_params=pltpu.CompilerParams(
            collective_id=0, has_side_effects=True, vmem_limit_bytes=60 * 1024 * 1024
        ),
        cost_estimate=pl.CostEstimate(
            flops=6 * hidden * feats * steps * points, bytes_accessed=4 * 1024 * 1024, transcendentals=hidden * steps * points
        ),
    )(
        latent, jnp.transpose(targets, (1, 0, 2)), w1, jnp.transpose(w2), noise_table, member_ids,
        lat_weight[None, :], area_index[None, :], var_weight[None, :],
    )
    return jnp.reshape(loss, (1,)), latent_grad, w1_grad, jnp.transpose(w2_grad)


def solution(mesh):
    return jax.shard_map(
        on_device if tuple(mesh.shape[a] for a in ("grid", "member")) != (4, 4) else fused_on_device,
        mesh=mesh,
        in_specs=(
            P(None, "member", None, ("rep", "grid")),
            P(None, None, ("rep", "grid")),
            P("grid", None),
            P(None, "grid"),
            P(),
            P(("rep", "member")),
            P(),
            P(("rep", "grid")),
            P(),
        ),
        out_specs=(
            P("rep"),
            P(None, "member", None, ("rep", "grid")),
            P(("rep", "grid"), None),
            P(None, ("rep", "grid")),
        ),
        check_vma=False,
    )
```
